512 devices in a mesh: lat: 16 (over y, x_lo, core), lon: 32 (over z, x_hi).
Axes of the slice: x: 4 (x_hi: 2, x_lo: 2; x = x_hi * 2 + x_lo), y: 4, z: 16, core: 2. Of those that a mesh axis runs over, the one named last changes fastest.
Arguments:
- field: float32 [69, 240, 1440], P(None, 'lat', 'lon'), may hold values from -6 to 6
- w_first: float32 [9, 128, 69], replicated, may hold values from -0.25 to 0.25
- b_first: float32 [128], replicated, may hold values from -3 to 3
- w_second: float32 [9, 128, 128], replicated, may hold values from -0.1875 to 0.1875
- b_second: float32 [128], replicated, may hold values from -3 to 3
- modes: float32 [512, 128], replicated, may hold values from -0.5 to 0.5
- cotangent: float32 [512], replicated, may hold values from -6 to 6
Outputs:
- grad_field: float32 [69, 240, 1440], P(None, 'lat', 'lon')
- grad_w_first: float32 [9, 128, 69], replicated
- grad_b_first: float32 [128], replicated
- grad_w_second: float32 [9, 128, 128], replicated
- grad_b_second: float32 [128], replicated
- grad_modes: float32 [512, 128], replicated
The draws below stay inside these ranges and needn't reach their ends.
All inputs are finite; a program needn't handle non-finite values.
Results may differ from the reference program's by a relative error of at most 0.00014.
Values sent between devices are 32-bit elements; how exact they have to be, the bound alone decides.
No kernel may reach another device: no remote copies, remote signals or barrier semaphores. Data moves between devices by JAX's collectives and lax.ppermute only.
A program may use at most 64 MiB of HBM per device.

```python
import math
import jax
import jax.numpy as jnp
from jax import lax

CIN = 69
CH = 128
MODES = 512
NLAT = 240
NLON = 1440


def block_levels(rng, extent, pieces, low, high):
    loudness = 1.0
    for position, blocks in pieces:
        steps = jax.random.uniform(jax.random.fold_in(jax.random.fold_in(rng, 6), position), (blocks,), jnp.float32, low / len(pieces), high / len(pieces))
        loudness = loudness * jnp.repeat(jnp.exp(steps), extent[position] // blocks).reshape((-1,) + (1,) * (len(extent) - 1 - position))
    return loudness


def centred(stream_key, extent, deviation, bound, pieces=(), kind=jnp.bfloat16):
    gain = block_levels(stream_key, extent, pieces, -0.22, 0.18) if pieces else 1.0
    entries = jax.random.normal(stream_key, extent, jnp.float32) * deviation * gain
    return jnp.minimum(jnp.maximum(entries, -bound), bound).astype(kind)


def setup_inputs(seed: int = 0) -> dict:
    key_list = jax.random.split(jax.random.key(seed), 8)
    return {
        "field": centred(key_list[0], (CIN, NLAT, NLON), 1.0, 6.0, ((1, 16), (2, 32)), jnp.float32),
        "w_first": centred(key_list[1], (9, CH, CIN), (9 * CIN) ** -0.5, 0.25, (), jnp.float32),
        "b_first": centred(key_list[2], (CH,), 0.5, 3.0, (), jnp.float32),
        "w_second": centred(key_list[3], (9, CH, CH), (9 * CH) ** -0.5, 0.1875, (), jnp.float32),
        "b_second": centred(key_list[4], (CH,), 0.5, 3.0, (), jnp.float32),
        "modes": centred(key_list[5], (MODES, CH), CH ** -0.5, 0.5, (), jnp.float32),
        "cotangent": centred(key_list[6], (MODES,), 1.0, 6.0, (), jnp.float32),
    }


def pad_grid(values):
    values = jnp.pad(values, ((0, 0), (1, 1), (0, 0)))
    return jnp.concatenate([values[:, :, -1:], values, values[:, :, :1]], axis=2)

def convolve(padded, weight, rows, cols):
    total = None
    for tap in range(9):
        shift_a, shift_b = (tap // 3, tap % 3)
        term = jnp.einsum('oc,chw->ohw', weight[tap], padded[:, shift_a:shift_a + rows, shift_b:shift_b + cols], precision=lax.Precision.HIGHEST)
        total = term if total is None else total + term
    return total

def area_weights():
    phi = (jnp.arange(NLAT, dtype=jnp.float32) + 0.5) * (math.pi / NLAT) - math.pi / 2
    cosine = jnp.cos(phi)
    return cosine / (jnp.sum(cosine) * NLON)

def forward(field, w_first, b_first, w_second, b_second, modes):
    hidden_one = convolve(pad_grid(field), w_first, NLAT, NLON) + b_first[:, None, None]
    active_one = jax.nn.silu(hidden_one)
    hidden_two = convolve(pad_grid(active_one), w_second, NLAT, NLON) + b_second[:, None, None]
    active_two = jax.nn.silu(hidden_two)
    pooled = jnp.einsum('chw,h->c', active_two, area_weights(), precision=lax.Precision.HIGHEST)
    amplitude = jnp.dot(modes, pooled, precision=lax.Precision.HIGHEST)
    spread = jnp.sqrt(jnp.mean(amplitude * amplitude) + 1e-05)
    return amplitude / spread

def reference(field, w_first, b_first, w_second, b_second, modes, cotangent):
    output, pullback = jax.vjp(forward, field, w_first, b_first, w_second, b_second, modes)
    grads = pullback(cotangent)
    return (grads[0] * float(NLAT * NLON), grads[1], grads[2], grads[3], grads[4], grads[5])
```

```python
import math

import jax
import jax.numpy as jnp
from jax import lax
from jax.sharding import Mesh, PartitionSpec as P

LAT = ("y", "xl", "c")
LON = ("z", "xh")
PLANE = ("y", "xl", "xh", "c")
RING = ("z",)
HIGH = lax.Precision.HIGH


def grow(cells, axes, dim, width, closed):
    count = lax.axis_size(axes)
    ends = count if closed else count - 1
    head = lax.slice_in_dim(cells, 0, width, axis=dim)
    tail = lax.slice_in_dim(cells, cells.shape[dim] - width, cells.shape[dim], axis=dim)
    return jnp.concatenate(
        [
            lax.ppermute(tail, axes, [(i, (i + 1) % count) for i in range(ends)]),
            cells,
            lax.ppermute(head, axes, [((i + 1) % count, i) for i in range(ends)]),
        ],
        axis=dim,
    )


def convolve(padded, weight, rows, cols):
    total = None
    for tap in range(9):
        a, b = tap // 3, tap % 3
        term = jnp.einsum("oc,chw->ohw", weight[tap], padded[:, a : a + rows, b : b + cols], precision=HIGH)
        total = term if total is None else total + term
    return total


def transpose_conv(padded, weight, rows, cols):
    total = None
    for tap in range(9):
        a, b = 2 - tap // 3, 2 - tap % 3
        term = jnp.einsum("oc,ohw->chw", weight[tap], padded[:, a : a + rows, b : b + cols], precision=HIGH)
        total = term if total is None else total + term
    return total


def kernel_grad(grad, padded, rows, cols, spec):
    return jnp.stack(
        [
            jnp.einsum(spec, grad, padded[:, t // 3 : t // 3 + rows, t % 3 : t % 3 + cols], precision=HIGH)
            for t in range(9)
        ]
    )


def slope(pre):
    sigma = jax.nn.sigmoid(pre)
    return sigma * (1.0 + pre * (1.0 - sigma))


def row_weights(first, count, nlat, nlon):
    every = (jnp.arange(nlat, dtype=jnp.float32) + 0.5) * (math.pi / nlat) - math.pi / 2
    total = jnp.sum(jnp.cos(every)) * nlon
    global_rows = first + jnp.arange(count, dtype=jnp.int32)
    phi = (global_rows.astype(jnp.float32) + 0.5) * (math.pi / nlat) - math.pi / 2
    inside = (global_rows >= 0) & (global_rows < nlat)
    return jnp.where(inside, jnp.cos(phi), 0.0) / total, inside


def swap(pieces, axes):
    return lax.all_to_all(pieces, axes, 0, 0, tiled=True)


def to_all(piece, axes):
    return swap(jnp.broadcast_to(piece[None], (lax.axis_size(axes),) + piece.shape), axes)


def fill(rows, count):
    return jnp.pad(rows, ((0, count - rows.shape[0]), (0, 0)))


def body(field, w_first, b_first, w_second, b_second, modes, cotangent):
    cin, rows, cols = field.shape
    ch = w_first.shape[1]
    n_lat, n_lon = lax.axis_size(LAT), lax.axis_size(LON)
    n_pl, n_z = lax.axis_size(PLANE), lax.axis_size(RING)
    nlat, nlon = rows * n_lat, cols * n_lon
    first = lax.axis_index(LAT) * rows

    fext = grow(grow(field, LAT, 1, 4, False), LON, 2, 4, True)
    weights, inside = row_weights(first - 3, rows + 6, nlat, nlon)
    inside = inside[None, :, None]
    h1 = convolve(fext, w_first, rows + 6, cols + 6) + b_first[:, None, None]
    a1 = jnp.where(inside, jax.nn.silu(h1), 0.0)
    s1 = jnp.where(inside, slope(h1), 0.0)[:, 2 : rows + 4, 2 : cols + 4]
    h2 = convolve(a1, w_second, rows + 4, cols + 4) + b_second[:, None, None]
    s2 = weights[None, 1 : rows + 5, None] * slope(h2)
    own_h2 = h2[:, 2 : rows + 2, 2 : cols + 2]
    own_s2 = s2[:, 2 : rows + 2, 2 : cols + 2]
    own_weights = weights[3 : rows + 3][None, :, None]
    pooled = jnp.sum(jax.nn.silu(own_h2) * own_weights, axis=(1, 2))
    bias2 = jnp.sum(own_s2, axis=(1, 2))
    g2 = kernel_grad(own_s2, a1[:, 2 : rows + 4, 2 : cols + 4], rows, cols, "ohw,chw->oc")

    share2 = 9 * ch // n_pl
    small = jnp.stack([pooled, bias2])
    part = jnp.concatenate(
        [g2.reshape(n_pl, share2, ch), jnp.broadcast_to(small[None], (n_pl, 2, ch))], axis=1
    )
    part = jnp.sum(swap(part, PLANE), axis=0)
    bit2 = -(-share2 // n_z)
    mine = fill(part[:share2], bit2 * n_z).reshape(n_z, bit2, ch)
    mine = jnp.concatenate([mine, jnp.broadcast_to(part[None, share2:], (n_z, 2, ch))], axis=1)
    mine = jnp.sum(swap(mine, RING), axis=0)
    piece2, pooled, bias2 = mine[:bit2], mine[bit2], mine[bit2 + 1]

    amplitude = jnp.dot(modes, pooled, precision=lax.Precision.HIGHEST)
    spread = jnp.sqrt(jnp.mean(amplitude * amplitude) + 1e-05)
    normal = amplitude / spread
    d_amplitude = (cotangent - normal * jnp.mean(cotangent * normal)) / spread
    d_modes = d_amplitude[:, None] * pooled[None, :]
    d_pooled = jnp.dot(d_amplitude, modes, precision=lax.Precision.HIGHEST)

    grad_two = d_pooled[:, None, None] * s2
    grad_one = transpose_conv(grad_two, w_second, rows + 2, cols + 2) * s1
    own_one = grad_one[:, 1 : rows + 1, 1 : cols + 1]
    g1 = kernel_grad(own_one, fext[:, 3 : rows + 5, 3 : cols + 5], rows, cols, "ohw,chw->co")
    bias1 = jnp.sum(own_one, axis=(1, 2))
    grad_field = transpose_conv(grad_one, w_first, rows, cols) * float(nlat * nlon)

    share1 = -(-(9 * cin + 1) // n_pl)
    part = fill(jnp.concatenate([g1.reshape(9 * cin, ch), bias1[None]]), share1 * n_pl)
    part = jnp.sum(swap(part.reshape(n_pl, share1, ch), PLANE), axis=0)
    both = to_all(jnp.concatenate([part, piece2]), RING)
    part = jnp.sum(both[:, :share1], axis=0)
    piece2 = both[:, share1:].reshape(n_z * bit2, ch)[:share2]
    whole = to_all(jnp.concatenate([piece2, part]), PLANE)
    grad_w_second = whole[:, :share2].reshape(9, ch, ch) * d_pooled[None, :, None]
    first_rows = whole[:, share2:].reshape(n_pl * share1, ch)
    grad_w_first = first_rows[: 9 * cin].reshape(9, cin, ch).transpose(0, 2, 1)
    return (grad_field, grad_w_first, first_rows[9 * cin], grad_w_second, bias2 * d_pooled, d_modes)


def solution(mesh):
    fine = Mesh(mesh.devices.reshape(4, 2, 2, 16, 2), ("y", "xl", "c", "z", "xh"))
    in_specs = (P(None, LAT, LON), P(), P(), P(), P(), P(), P())
    out_specs = (P(None, LAT, LON), P(), P(), P(), P(), P())
    return jax.shard_map(body, mesh=fine, in_specs=in_specs, out_specs=out_specs, check_vma=False)
```

```python
import math

import jax
import jax.numpy as jnp
from jax import lax
from jax.experimental import pallas as pl
from jax.experimental.pallas import tpu as pltpu
from jax.sharding import Mesh, PartitionSpec as P

LAT = ("y", "xl", "c")
LON = ("z", "xh")
PLANE = ("y", "xl", "xh", "c")
RING = ("z",)
F32 = jnp.float32
BF16 = jnp.bfloat16

PITCH = 64
LANES = 128
ROWS, COLS, CIN = 15, 45, 69
WINDOW = 16 * PITCH
NX, N1, N2, N3 = 23 * PITCH, 21 * PITCH, 19 * PITCH, 17 * PITCH


def split(x):
    hi = x.astype(BF16)
    return hi, (x - hi.astype(F32)).astype(BF16)


def spread(src, high, low, start, stop):
    for r in range(start, stop, PITCH):
        for b in range(3):
            hi, lo = split(src[r + b : r + b + PITCH, :])
            high[r : r + PITCH, b * LANES : (b + 1) * LANES] = hi
            low[r : r + PITCH, b * LANES : (b + 1) * LANES] = lo


def dot(a, b):
    return jnp.dot(a, b, preferred_element_type=F32)


def convolve(high, low, weight, start, count):
    total = None
    for a in range(3):
        r = start + a * PITCH
        w = weight[a]
        both = dot(high[r : r + count, :], w)
        term = both[:, :LANES] + both[:, LANES:] + dot(low[r : r + count, :], w[:, :LANES])
        total = term if total is None else total + term
    return total


def correlate(grad, high, low, start):
    hi, lo = split(grad.T)
    both = jnp.concatenate([hi, lo], axis=0)
    blocks = []
    for a in range(3):
        r = start + a * PITCH
        x = high[r : r + WINDOW, :]
        out = dot(both, x)
        blocks.append(out[:LANES] + out[LANES:] + dot(hi, low[r : r + WINDOW, :]))
    return blocks


def chunks(rows, parts):
    size = -(-rows // parts)
    return [(s, min(size, rows - s)) for s in range(0, rows, size)]


def column_mask(first, shape):
    col = lax.broadcasted_iota(jnp.int32, shape, 0)
    return ((col >= first) & (col < first + COLS)).astype(F32)


def forward_kernel(weights, own, north, south, west, east, w1, b1, w2, b2, x, a1, s1, s2, small, high, low):
    x[...] = jnp.zeros_like(x)
    for i in range(ROWS + 8):
        r = i * PITCH
        row = north[i] if i < 4 else own[i - 4] if i < ROWS + 4 else south[i - ROWS - 4]
        x[r + 8 : r + 8 + COLS, :CIN] = row
        x[r + 4 : r + 8, :CIN] = west[i]
        x[r + 8 + COLS : r + 12 + COLS, :CIN] = east[i]
    spread(x, high, low, 0, NX)
    for first, rows in chunks(ROWS + 6, 3):
        acc = convolve(high, low, w1, first * PITCH, rows * PITCH)
        for k in range(rows):
            r = (first + k) * PITCH
            h = acc[k * PITCH : (k + 1) * PITCH] + b1[...]
            sigma = jax.nn.sigmoid(h)
            inside = jnp.where(weights[first + k] > 0.0, 1.0, 0.0)
            a1[r : r + PITCH, :] = h * sigma * inside
            s1[r : r + PITCH, :] = sigma * (1.0 + h * (1.0 - sigma)) * inside
    a1[N1:, :] = jnp.zeros((8, LANES), F32)
    s1[N1:, :] = jnp.zeros((8, LANES), F32)
    spread(a1, high, low, 0, N1)
    mask = column_mask(6, (PITCH, LANES))
    pooled = jnp.zeros((PITCH, LANES), F32)
    bias = jnp.zeros((PITCH, LANES), F32)
    for first, rows in chunks(ROWS + 4, 2):
        acc = convolve(high, low, w2, first * PITCH, rows * PITCH)
        for k in range(rows):
            i = first + k
            r = i * PITCH
            h = acc[k * PITCH : (k + 1) * PITCH] + b2[...]
            sigma = jax.nn.sigmoid(h)
            weight = weights[i + 1]
            slope = sigma * (1.0 + h * (1.0 - sigma)) * weight
            s2[r : r + PITCH, :] = slope
            if 2 <= i < ROWS + 2:
                pooled = pooled + h * sigma * weight
                bias = bias + slope
    s2[N2:, :] = jnp.zeros((8, LANES), F32)
    small[0:1, :] = jnp.sum(pooled * mask, axis=0, keepdims=True)
    small[1:2, :] = jnp.sum(bias * mask, axis=0, keepdims=True)


def second_kernel(a1, s2, out, high, low, rows):
    spread(a1, high, low, 2 * PITCH, 20 * PITCH)
    mask = column_mask(6, (PITCH, LANES))
    own = [s2[(i + 2) * PITCH : (i + 3) * PITCH, :] * mask for i in range(ROWS)]
    grad = jnp.concatenate(own + [jnp.zeros((PITCH, LANES), F32)], axis=0)
    for a, block in enumerate(correlate(grad, high, low, 2 * PITCH)):
        for b in range(3):
            t = 3 * a + b
            rows[t * LANES : (t + 1) * LANES, :] = block[:, b * LANES : (b + 1) * LANES]
    size = out.shape[1]
    for p in range(out.shape[0]):
        out[p] = rows[p * size : (p + 1) * size, :]


def backward_kernel(sums, modes, cot, s2, s1, x, w2, out, d_modes, spread_d, bias2, g1, g2, high, low, rows):
    total = jnp.sum(sums[...], axis=0)
    pooled = total[0:1]
    amplitude = jnp.sum(modes[...] * pooled, axis=1, keepdims=True)
    count = amplitude.shape[0]
    width = jnp.sqrt(jnp.sum(amplitude * amplitude, axis=0, keepdims=True) / count + 1e-05)
    normal = amplitude / width
    along = jnp.sum(cot[...] * normal, axis=0, keepdims=True) / count
    d_amplitude = (cot[...] - normal * along) / width
    d_modes[...] = d_amplitude * pooled
    d_pooled = jnp.sum(d_amplitude * modes[...], axis=0, keepdims=True)
    spread_d[...] = jnp.broadcast_to(d_pooled, (LANES, LANES)).T
    bias2[...] = total[1:2] * d_pooled

    for i in range(ROWS + 4):
        r = i * PITCH
        g2[r : r + PITCH, :] = s2[r : r + PITCH, :] * d_pooled
    g2[N2:, :] = jnp.zeros((8, LANES), F32)
    spread(g2, high, low, 0, N2)
    for first, count in chunks(ROWS + 2, 2):
        r, n = first * PITCH, count * PITCH
        g1[r : r + n, :] = convolve(high, low, w2, r, n) * s1[r + 2 * PITCH + 2 : r + 2 * PITCH + 2 + n, :]
    g1[N3:, :] = jnp.zeros((8, LANES), F32)

    mask = column_mask(7, (PITCH, LANES))
    own = [g1[(i + 1) * PITCH - 2 : (i + 2) * PITCH - 2, :] * mask for i in range(ROWS)]
    bias1 = own[0]
    for row in own[1:]:
        bias1 = bias1 + row
    grad = jnp.concatenate(own + [jnp.zeros((PITCH, LANES), F32)], axis=0)
    spread(x, high, low, 3 * PITCH, 21 * PITCH)
    for a, block in enumerate(correlate(grad, high, low, 3 * PITCH)):
        for b in range(3):
            t = 3 * a + b
            rows[t * CIN : (t + 1) * CIN, :] = block[:, b * LANES : (b + 1) * LANES].T[:CIN]
    rows[9 * CIN : 9 * CIN + 1, :] = jnp.sum(bias1, axis=0, keepdims=True)
    rows[9 * CIN + 1 :, :] = jnp.zeros((rows.shape[0] - 9 * CIN - 1, LANES), F32)
    size = out.shape[1]
    for p in range(out.shape[0]):
        out[p] = rows[p * size : (p + 1) * size, :]


def field_kernel(scale, g1, w1, out, high, low):
    spread(g1, high, low, 0, N3)
    for first, count in chunks(ROWS, 2):
        acc = convolve(high, low, w1, first * PITCH, count * PITCH) * scale
        for k in range(count):
            out[first + k] = acc[k * PITCH + 4 : k * PITCH + 4 + COLS, :CIN]


def finish_kernel(whole, spread_d, w_second, w_first, b_first, rows):
    pieces, size = whole.shape[0], 9 * LANES // whole.shape[0]
    rest = whole.shape[1] - size
    for p in range(pieces):
        rows[p * size : (p + 1) * size, :] = whole[p, :size, :]
    for t in range(9):
        w_second[t] = rows[t * LANES : (t + 1) * LANES, :] * spread_d[...]
    for p in range(pieces):
        rows[p * rest : (p + 1) * rest, :] = whole[p, size:, :]
    for t in range(9):
        w_first[t] = rows[t * CIN : t * CIN + LANES, :].T[:, :CIN]
    b_first[...] = rows[9 * CIN : 9 * CIN + 1, :]


def call(kernel, outs, scratch, flops, smem=()):
    def run(*args):
        ins = [pl.BlockSpec(memory_space=pltpu.SMEM if i in smem else pltpu.VMEM) for i in range(len(args))]
        return pl.pallas_call(
            kernel,
            out_shape=[jax.ShapeDtypeStruct(s, F32) for s in outs],
            in_specs=ins,
            out_specs=[pl.BlockSpec(memory_space=pltpu.VMEM) for _ in outs],
            scratch_shapes=[pltpu.VMEM(s, d) for s, d in scratch],
            compiler_params=pltpu.CompilerParams(vmem_limit_bytes=32 << 20),
            cost_estimate=pl.CostEstimate(flops=flops, bytes_accessed=4 << 20, transcendentals=0),
        )(*args)

    return run


def stacked(weight, flip):
    weight = weight[::-1] if flip else weight
    weight = jnp.pad(weight, ((0, 0), (0, LANES - weight.shape[1]), (0, LANES - weight.shape[2])))
    weight = weight.reshape(3, 3 * LANES, LANES)
    high = lax.reduce_precision(weight, 8, 7)
    return jnp.concatenate([high.astype(BF16), (weight - high).astype(BF16)], axis=2)


def edges(cells, axes, dim, width, closed):
    count = lax.axis_size(axes)
    ends = count if closed else count - 1
    head = lax.slice_in_dim(cells, 0, width, axis=dim)
    tail = lax.slice_in_dim(cells, cells.shape[dim] - width, cells.shape[dim], axis=dim)
    before = lax.ppermute(tail, axes, [(i, (i + 1) % count) for i in range(ends)])
    after = lax.ppermute(head, axes, [((i + 1) % count, i) for i in range(ends)])
    return before, after


def row_weights(first, count, nlat, nlon):
    every = (jnp.arange(nlat, dtype=F32) + 0.5) * (math.pi / nlat) - math.pi / 2
    total = jnp.sum(jnp.cos(every)) * nlon
    global_rows = first + jnp.arange(count, dtype=jnp.int32)
    phi = (global_rows.astype(F32) + 0.5) * (math.pi / nlat) - math.pi / 2
    inside = (global_rows >= 0) & (global_rows < nlat)
    return jnp.where(inside, jnp.cos(phi), 0.0) / total


def swap(pieces, axes):
    return lax.all_to_all(pieces, axes, 0, 0, tiled=True)


def to_all(piece, axes):
    return swap(jnp.broadcast_to(piece[None], (lax.axis_size(axes),) + piece.shape), axes)


def fill(rows, count):
    return jnp.pad(rows, ((0, count - rows.shape[0]), (0, 0)))


def body(field, w_first, b_first, w_second, b_second, modes, cotangent):
    cin, rows, cols = field.shape
    ch = w_first.shape[1]
    n_lat, n_lon = lax.axis_size(LAT), lax.axis_size(LON)
    n_pl, n_z = lax.axis_size(PLANE), lax.axis_size(RING)
    nlat, nlon = rows * n_lat, cols * n_lon
    weights = row_weights(lax.axis_index(LAT) * rows - 3, 24, nlat, nlon)

    own = field.transpose(1, 2, 0)
    north, south = edges(own, LAT, 0, 4, False)
    left = jnp.concatenate([north[:, :4], own[:, :4], south[:, :4]], axis=0)
    right = jnp.concatenate([north[:, cols - 4 :], own[:, cols - 4 :], south[:, cols - 4 :]], axis=0)
    west, east = edges(jnp.concatenate([left, right], axis=1), LON, 1, 4, True)

    w1 = stacked(w_first.transpose(0, 2, 1), False)
    w2 = stacked(w_second.transpose(0, 2, 1), False)
    w2_back = stacked(w_second, True)
    w1_back = stacked(w_first, True)

    three = (3 * LANES,)
    pair = lambda n: [((n,) + three, BF16), ((n,) + three, BF16)]
    x, a1, s1, s2, small = call(
        forward_kernel,
        [(NX + 8, LANES), (N1 + 8, LANES), (N1 + 8, LANES), (N2 + 8, LANES), (2, LANES)],
        pair(NX),
        10**9,
        (0,),
    )(weights, own, north, south, west, east, w1, b_first[None], w2, b_second[None])

    share2 = 9 * ch // n_pl
    (g2,) = call(second_kernel, [(n_pl, share2, ch)], pair(20 * PITCH) + [((9 * ch, LANES), F32)], 10**9)(a1, s2)

    part = jnp.concatenate([g2, jnp.broadcast_to(small[None], (n_pl, 2, ch))], axis=1)
    part = jnp.sum(swap(part, PLANE), axis=0)
    bit2 = -(-share2 // n_z)
    mine = fill(part[:share2], bit2 * n_z).reshape(n_z, bit2, ch)
    mine = jnp.concatenate([jnp.broadcast_to(part[None, share2:], (n_z, 2, ch)), mine], axis=1)
    mine = swap(mine, RING)
    piece2 = jnp.sum(mine[:, 2:], axis=0)

    share1 = -(-(9 * cin + 1) // n_pl)
    g1rows, d_modes, spread_d, bias2, g1 = call(
        backward_kernel,
        [(n_pl, share1, ch), modes.shape, (LANES, LANES), (1, LANES), (N3 + 8, LANES)],
        [((N2 + 8, LANES), F32)] + pair(21 * PITCH) + [((n_pl * share1, LANES), F32)],
        10**9,
    )(mine, modes, cotangent[:, None], s2, s1, x, w2_back)

    part = jnp.sum(swap(g1rows, PLANE), axis=0)
    (grad_field,) = call(lambda *r: field_kernel(float(nlat * nlon), *r), [(rows, cols, cin)], pair(N3), 10**9)(g1, w1_back)

    both = to_all(jnp.concatenate([part, piece2]), RING)
    part = jnp.sum(both[:, :share1], axis=0)
    piece2 = both[:, share1:].reshape(n_z * bit2, ch)[:share2]
    whole = to_all(jnp.concatenate([piece2, part]), PLANE)
    grad_w_second, grad_w_first, grad_b_first = call(
        finish_kernel,
        [(9, ch, ch), (9, ch, cin), (1, ch)],
        [((9 * ch, LANES), F32)],
        10**6,
    )(whole, spread_d)
    return (grad_field.transpose(2, 0, 1), grad_w_first, grad_b_first[0], grad_w_second, bias2[0], d_modes)


def solution(mesh):
    fine = Mesh(mesh.devices.reshape(4, 2, 2, 16, 2), ("y", "xl", "c", "z", "xh"))
    in_specs = (P(None, LAT, LON), P(), P(), P(), P(), P(), P())
    out_specs = (P(None, LAT, LON), P(), P(), P(), P(), P())
    return jax.shard_map(body, mesh=fine, in_specs=in_specs, out_specs=out_specs, check_vma=False)
```

```python
import math

import jax
import jax.numpy as jnp
import numpy as np
from jax import lax
from jax.experimental import pallas as pl
from jax.experimental.pallas import tpu as pltpu
from jax.sharding import Mesh, PartitionSpec as P

LAT = ("y", "xl", "c")
LON = ("z", "xh")
CHIPS = ("y", "xl", "xh")
PLANE = ("y", "xl", "xh", "c")
RING = ("z",)
F32 = jnp.float32
BF16 = jnp.bfloat16

PITCH = 64
LANES = 128
ROWS, COLS, CIN = 15, 45, 69
WINDOW = 16 * PITCH
NX, N1, N2, N3 = 23 * PITCH, 21 * PITCH, 19 * PITCH, 17 * PITCH


def split(x):
    hi = x.astype(BF16)
    return hi, (x - hi.astype(F32)).astype(BF16)


def spread(src, high, low, start, stop):
    for r in range(start, stop, PITCH):
        for b in range(3):
            hi, lo = split(src[r + b : r + b + PITCH, :])
            high[r : r + PITCH, b * LANES : (b + 1) * LANES] = hi
            low[r : r + PITCH, b * LANES : (b + 1) * LANES] = lo


def dot(a, b):
    return jnp.dot(a, b, preferred_element_type=F32)


def convolve(high, low, weight, start, count):
    total = None
    for a in range(3):
        r = start + a * PITCH
        w = weight[a]
        both = dot(high[r : r + count, :], w)
        term = both[:, :LANES] + both[:, LANES:] + dot(low[r : r + count, :], w[:, :LANES])
        total = term if total is None else total + term
    return total


def correlate(grad, high, low, start):
    hi, lo = split(grad.T)
    both = jnp.concatenate([hi, lo], axis=0)
    blocks = []
    for a in range(3):
        r = start + a * PITCH
        x = high[r : r + WINDOW, :]
        out = dot(both, x)
        blocks.append(out[:LANES] + out[LANES:] + dot(hi, low[r : r + WINDOW, :]))
    return blocks


def chunks(rows, parts):
    size = -(-rows // parts)
    return [(s, min(size, rows - s)) for s in range(0, rows, size)]


def column_mask(first, shape):
    col = lax.broadcasted_iota(jnp.int32, shape, 0)
    return ((col >= first) & (col < first + COLS)).astype(F32)


def padded_rows(pad, block):
    pad[:CIN, :] = block
    return pad[...]


def store_weight(weight, t, block):
    a, b = t // 3, t % 3
    hi, lo = split(block)
    weight[a, b * LANES : (b + 1) * LANES, :LANES] = hi
    weight[a, b * LANES : (b + 1) * LANES, LANES:] = lo


def prepare_kernel(own, north, south, w_first, w_second, x, w1, w2, pad):
    x[...] = jnp.zeros_like(x)
    for i in range(ROWS + 8):
        r = i * PITCH
        row = north[i] if i < 4 else own[i - 4] if i < ROWS + 4 else south[i - ROWS - 4]
        x[r + 8 : r + 8 + COLS, :CIN] = row
    pad[...] = jnp.zeros_like(pad)
    for t in range(9):
        store_weight(w1, t, padded_rows(pad, w_first[t]))
        store_weight(w2, t, w_second[t].T)


def forward_kernel(weights, centre, west, east, w1, b1, w2, b2, cells, a1, s1, s2, small, x, slopes, high, low):
    x[...] = centre[...]
    for i in range(ROWS + 8):
        r = i * PITCH
        x[r + 4 : r + 8, :CIN] = west[i]
        x[r + 8 + COLS : r + 12 + COLS, :CIN] = east[i]
    spread(x, high, low, 0, NX)
    cells[...] = x[3 * PITCH : 21 * PITCH + 8, :]
    for first, rows in chunks(ROWS + 6, 3):
        acc = convolve(high, low, w1, first * PITCH, rows * PITCH)
        for k in range(rows):
            r = (first + k) * PITCH
            h = acc[k * PITCH : (k + 1) * PITCH] + b1[...]
            sigma = jax.nn.sigmoid(h)
            inside = jnp.where(weights[first + k] > 0.0, 1.0, 0.0)
            a1[r : r + PITCH, :] = h * sigma * inside
            slopes[r : r + PITCH, :] = sigma * (1.0 + h * (1.0 - sigma)) * inside
    a1[N1:, :] = jnp.zeros((8, LANES), F32)
    s1[...] = slopes[2 * PITCH + 2 : 2 * PITCH + 2 + N3, :]
    spread(a1, high, low, 0, N1)
    mask = column_mask(6, (PITCH, LANES))
    pooled = jnp.zeros((PITCH, LANES), F32)
    bias = jnp.zeros((PITCH, LANES), F32)
    for first, rows in chunks(ROWS + 4, 2):
        acc = convolve(high, low, w2, first * PITCH, rows * PITCH)
        for k in range(rows):
            i = first + k
            r = i * PITCH
            h = acc[k * PITCH : (k + 1) * PITCH] + b2[...]
            sigma = jax.nn.sigmoid(h)
            weight = weights[i + 1]
            slope = sigma * (1.0 + h * (1.0 - sigma)) * weight
            s2[r : r + PITCH, :] = slope
            if 2 <= i < ROWS + 2:
                pooled = pooled + h * sigma * weight
                bias = bias + slope
    s2[N2:, :] = jnp.zeros((8, LANES), F32)
    small[0:1, :] = jnp.sum(pooled * mask, axis=0, keepdims=True)
    small[1:2, :] = jnp.sum(bias * mask, axis=0, keepdims=True)


def write_pieces(out, rows, extra=None):
    count, size = out.shape[0], out.shape[1] - (0 if extra is None else extra.shape[0])
    for p in range(count):
        q = (p % 2) * (count // 2) + p // 2
        out[p, :size] = rows[q * size : (q + 1) * size, :]
        if extra is not None:
            out[p, size:] = extra[...]


def second_kernel(a1, s2, small, out, high, low, rows):
    spread(a1, high, low, 2 * PITCH, 20 * PITCH)
    mask = column_mask(6, (PITCH, LANES))
    own = [s2[(i + 2) * PITCH : (i + 3) * PITCH, :] * mask for i in range(ROWS)]
    grad = jnp.concatenate(own + [jnp.zeros((PITCH, LANES), F32)], axis=0)
    for a, block in enumerate(correlate(grad, high, low, 2 * PITCH)):
        for b in range(3):
            t = 3 * a + b
            rows[t * LANES : (t + 1) * LANES, :] = block[:, b * LANES : (b + 1) * LANES]
    write_pieces(out, rows, small)


def mode_gradients(sums, modes, cot):
    total = jnp.sum(sums[...], axis=0)
    pooled = total[0:1]
    amplitude = jnp.sum(modes[...] * pooled, axis=1, keepdims=True)
    count = amplitude.shape[0]
    column = jnp.concatenate(
        [jnp.broadcast_to(cot[k : k + 1, :], (LANES, LANES)).T[:, :1] for k in range(count // LANES)], axis=0
    )
    width = jnp.sqrt(jnp.sum(amplitude * amplitude, axis=0, keepdims=True) / count + 1e-05)
    normal = amplitude / width
    along = jnp.sum(column * normal, axis=0, keepdims=True) / count
    d_amplitude = (column - normal * along) / width
    d_pooled = jnp.sum(d_amplitude * modes[...], axis=0, keepdims=True)
    return total, pooled, d_amplitude, d_pooled


def backward_kernel(sums, modes, cot, s1, s2, x, w_second, out, g1, weight, rows, high, low):
    spread(s2, high, low, 0, N2)
    d_pooled = mode_gradients(sums, modes, cot)[3]
    column = jnp.broadcast_to(d_pooled, (LANES, LANES)).T
    for t in range(9):
        store_weight(weight, t, w_second[8 - t] * column)
    for first, count in chunks(ROWS + 2, 2):
        r, n = first * PITCH, count * PITCH
        g1[r : r + n, :] = convolve(high, low, weight, r, n) * s1[r : r + n, :]
    g1[N3:, :] = jnp.zeros((8, LANES), F32)

    mask = column_mask(7, (PITCH, LANES))
    own = [g1[(i + 1) * PITCH - 2 : (i + 2) * PITCH - 2, :] * mask for i in range(ROWS)]
    bias1 = own[0]
    for row in own[1:]:
        bias1 = bias1 + row
    grad = jnp.concatenate(own + [jnp.zeros((PITCH, LANES), F32)], axis=0)
    spread(x, high, low, 0, 18 * PITCH)
    for a, block in enumerate(correlate(grad, high, low, 0)):
        for b in range(3):
            t = 3 * a + b
            rows[t * CIN : (t + 1) * CIN, :] = block[:, b * LANES : (b + 1) * LANES].T[:CIN]
    rows[9 * CIN : 9 * CIN + 1, :] = jnp.sum(bias1, axis=0, keepdims=True)
    rows[9 * CIN + 1 :, :] = jnp.zeros((rows.shape[0] - 9 * CIN - 1, LANES), F32)
    write_pieces(out, rows)


def field_kernel(scale, g1, w_first, sums, modes, cot, out, d_modes, spread_d, bias2, weight, pad, high, low):
    total, pooled, d_amplitude, d_pooled = mode_gradients(sums, modes, cot)
    d_modes[...] = d_amplitude * pooled
    spread_d[...] = jnp.broadcast_to(d_pooled, (LANES, LANES)).T
    bias2[...] = total[1:2] * d_pooled
    pad[...] = jnp.zeros_like(pad)
    for t in range(9):
        store_weight(weight, t, padded_rows(pad, w_first[8 - t]).T)
    spread(g1, high, low, 0, N3)
    for first, count in chunks(ROWS, 2):
        acc = convolve(high, low, weight, first * PITCH, count * PITCH) * scale
        for k in range(count):
            out[first + k] = acc[k * PITCH + 4 : k * PITCH + 4 + COLS, :CIN]


def finish_kernel(core, mine, other, spread_d, w_second, w_first, b_first, rows):
    chips = mine.shape[0]
    size = 9 * LANES // (2 * chips)
    rest = mine.shape[1] - size
    even = core[0] == 0

    def gather(start, count):
        for p in range(chips):
            m, o = mine[p, start : start + count, :], other[p, start : start + count, :]
            rows[p * count : (p + 1) * count, :] = jnp.where(even, m, o)
            rows[(chips + p) * count : (chips + p + 1) * count, :] = jnp.where(even, o, m)

    gather(0, size)
    for t in range(9):
        w_second[t] = rows[t * LANES : (t + 1) * LANES, :] * spread_d[...]
    gather(size, rest)
    for t in range(9):
        w_first[t] = rows[t * CIN : (t + 1) * CIN, :]
    b_first[...] = rows[9 * CIN : 9 * CIN + 1, :]


def call(kernel, outs, scratch, flops, smem=()):
    outs = [o if isinstance(o[0], tuple) else (o, F32) for o in outs]

    def run(*args):
        ins = [pl.BlockSpec(memory_space=pltpu.SMEM if i in smem else pltpu.VMEM) for i in range(len(args))]
        return pl.pallas_call(
            kernel,
            out_shape=[jax.ShapeDtypeStruct(s, d) for s, d in outs],
            in_specs=ins,
            out_specs=[pl.BlockSpec(memory_space=pltpu.VMEM) for _ in outs],
            scratch_shapes=[pltpu.VMEM(s, d) for s, d in scratch],
            compiler_params=pltpu.CompilerParams(vmem_limit_bytes=12 << 20),
            cost_estimate=pl.CostEstimate(flops=flops, bytes_accessed=4 << 20, transcendentals=0),
        )(*args)

    return run


def edges(cells, axes, dim, width, closed):
    count = lax.axis_size(axes)
    ends = count if closed else count - 1
    head = lax.slice_in_dim(cells, 0, width, axis=dim)
    tail = lax.slice_in_dim(cells, cells.shape[dim] - width, cells.shape[dim], axis=dim)
    before = lax.ppermute(tail, axes, [(i, (i + 1) % count) for i in range(ends)])
    after = lax.ppermute(head, axes, [((i + 1) % count, i) for i in range(ends)])
    return before, after


def row_weights(first, count, nlat, nlon):
    phi = (np.arange(nlat) + 0.5) * (math.pi / nlat) - math.pi / 2
    area = np.cos(phi) / (np.cos(phi).sum() * nlon)
    table = np.zeros(nlat + 2 * count, np.float32)
    table[count : count + nlat] = area
    return lax.dynamic_slice(jnp.asarray(table), (first + count,), (count,))


def swap(pieces, axes):
    return lax.all_to_all(pieces, axes, 0, 0, tiled=True)


def to_all(piece, axes):
    return swap(jnp.broadcast_to(piece[None], (lax.axis_size(axes),) + piece.shape), axes)


def fill(rows, count):
    return jnp.pad(rows, ((0, count - rows.shape[0]), (0, 0)))


def body(field, w_first, b_first, w_second, b_second, modes, cotangent):
    cin, rows, cols = field.shape
    ch = w_first.shape[1]
    n_lat, n_lon = lax.axis_size(LAT), lax.axis_size(LON)
    n_pl, n_z = lax.axis_size(PLANE), lax.axis_size(RING)
    nlat, nlon = rows * n_lat, cols * n_lon
    weights = row_weights(lax.axis_index(LAT) * rows - 3, 24, nlat, nlon)

    own = field.transpose(1, 2, 0)
    north, south = edges(own, LAT, 0, 4, False)
    left = jnp.concatenate([north[:, :4], own[:, :4], south[:, :4]], axis=0)
    right = jnp.concatenate([north[:, cols - 4 :], own[:, cols - 4 :], south[:, cols - 4 :]], axis=0)
    west, east = edges(jnp.concatenate([left, right], axis=1), LON, 1, 4, True)
    w_first = w_first.transpose(0, 2, 1)
    weight = ((3, 3 * LANES, 2 * LANES), BF16)
    pad = ((LANES, LANES), F32)
    pair = lambda n: [((n, 3 * LANES), BF16), ((n, 3 * LANES), BF16)]
    centre, w1, w2 = call(prepare_kernel, [(NX + 8, LANES), weight, weight], [pad], 10**9)(own, north, south, w_first, w_second)
    x, a1, s1, s2, small = call(
        forward_kernel,
        [(18 * PITCH + 8, LANES), (N1 + 8, LANES), (N3, LANES), (N2 + 8, LANES), (2, LANES)],
        [((NX + 8, LANES), F32), ((N1, LANES), F32)] + pair(NX),
        10**9,
        (0,),
    )(weights, centre, west, east, w1, b_first[None], w2, b_second[None])

    share2 = 9 * ch // n_pl
    (part,) = call(second_kernel, [(n_pl, share2 + 2, ch)], pair(20 * PITCH) + [((9 * ch, LANES), F32)], 10**9)(a1, s2, small)

    part = jnp.sum(swap(part, PLANE), axis=0)
    bit2 = -(-share2 // n_z)
    mine = fill(part[:share2], bit2 * n_z).reshape(n_z, bit2, ch)
    mine = jnp.concatenate([jnp.broadcast_to(part[None, share2:], (n_z, 2, ch)), mine], axis=1)
    mine = swap(mine, RING)
    piece2 = jnp.sum(mine[:, 2:], axis=0)

    share1 = -(-(9 * cin + 1) // n_pl)
    cot = cotangent.reshape(-1, LANES)
    g1rows, g1 = call(
        backward_kernel,
        [(n_pl, share1, ch), (N3 + 8, LANES)],
        [weight, ((n_pl * share1, LANES), F32)] + pair(N2),
        10**9,
    )(mine, modes, cot, s1, s2, x, w_second)

    part = jnp.sum(swap(g1rows, PLANE), axis=0)
    grad_field, d_modes, spread_d, bias2 = call(
        lambda *r: field_kernel(float(nlat * nlon), *r),
        [(rows, cols, cin), modes.shape, (LANES, LANES), (1, LANES)],
        [weight, pad] + pair(N3),
        10**9,
    )(g1, w_first, mine, modes, cot)
    part, grad_field = lax.optimization_barrier((part, grad_field))

    both = to_all(jnp.concatenate([part, piece2]), RING)
    part = jnp.sum(both[:, :share1], axis=0)
    piece2 = both[:, share1:].reshape(n_z * bit2, ch)[:share2]
    whole = to_all(jnp.concatenate([piece2, part]), CHIPS)
    other = lax.ppermute(whole, "c", [(0, 1), (1, 0)])
    core = lax.axis_index("c").astype(jnp.int32).reshape(1)
    grad_w_second, grad_w_first, grad_b_first = call(
        finish_kernel,
        [(9, ch, ch), (9, cin, ch), (1, ch)],
        [((9 * ch, LANES), F32)],
        10**6,
        (0,),
    )(core, whole, other, spread_d)
    return (grad_field.transpose(2, 0, 1), grad_w_first.transpose(0, 2, 1), grad_b_first[0], grad_w_second, bias2[0], d_modes)


def solution(mesh):
    fine = Mesh(mesh.devices.reshape(4, 2, 2, 16, 2), ("y", "xl", "c", "z", "xh"))
    in_specs = (P(None, LAT, LON), P(), P(), P(), P(), P(), P())
    out_specs = (P(None, LAT, LON), P(), P(), P(), P(), P())
    return jax.shard_map(body, mesh=fine, in_specs=in_specs, out_specs=out_specs, check_vma=False)
```

```python
import math

import jax
import jax.numpy as jnp
import numpy as np
from jax import lax
from jax.experimental import pallas as pl
from jax.experimental.pallas import tpu as pltpu
from jax.sharding import Mesh, PartitionSpec as P

LAT = ("y", "xl", "c")
LON = ("z", "xh")
CHIPS = ("y", "xl", "xh")
PLANE = ("y", "xl", "xh", "c")
RING = ("z",)
F32 = jnp.float32
BF16 = jnp.bfloat16

PITCH = 64
LANES = 128
ROWS, COLS, CIN = 15, 45, 69
WINDOW = 16 * PITCH
NX, N1, N2, N3 = 23 * PITCH, 21 * PITCH, 19 * PITCH, 17 * PITCH


def split(x):
    hi = x.astype(BF16)
    return hi, (x - hi.astype(F32)).astype(BF16)


def spread(src, high, low, start, stop):
    for r in range(start, stop, PITCH):
        for b in range(3):
            hi, lo = split(src[r + b : r + b + PITCH, :])
            high[r : r + PITCH, b * LANES : (b + 1) * LANES] = hi
            low[r : r + PITCH, b * LANES : (b + 1) * LANES] = lo


def spread_packed(src, high, low, start, stop):
    lane = lax.broadcasted_iota(jnp.int32, (PITCH, LANES), 1)
    for r in range(start, stop, PITCH):
        second = pltpu.roll(src[r + 1 : r + 1 + PITCH, :], CIN, 1)
        third = pltpu.roll(src[r + 2 : r + 2 + PITCH, :], 2 * CIN - LANES, 1)
        for k, x in enumerate(
            (jnp.where(lane < CIN, src[r : r + PITCH, :], second), jnp.where(lane < 2 * CIN - LANES, second, third))
        ):
            hi, lo = split(x)
            high[r : r + PITCH, k * LANES : (k + 1) * LANES] = hi
            low[r : r + PITCH, k * LANES : (k + 1) * LANES] = lo


def dot(a, b):
    return jnp.dot(a, b, preferred_element_type=F32)


def convolve(high, low, weight, start, count):
    def taps(src):
        return jnp.concatenate([src[start + a * PITCH : start + a * PITCH + count, :] for a in range(3)], axis=1)

    w = jnp.concatenate([weight[a] for a in range(3)], axis=0)
    both = dot(taps(high), w)
    return both[:, :LANES] + both[:, LANES:] + dot(taps(low), w[:, :LANES])


def correlate(grad, high, low, start):
    hi, lo = split(grad.T)
    both = jnp.concatenate([hi, lo], axis=0)
    blocks = []
    for a in range(3):
        r = start + a * PITCH
        x = high[r : r + WINDOW, :]
        out = dot(both, x)
        blocks.append(out[:LANES] + out[LANES:] + dot(hi, low[r : r + WINDOW, :]))
    return blocks


def chunks(rows, parts):
    size = -(-rows // parts)
    return [(s, min(size, rows - s)) for s in range(0, rows, size)]


def column_mask(first, shape):
    col = lax.broadcasted_iota(jnp.int32, shape, 0)
    return ((col >= first) & (col < first + COLS)).astype(F32)


def padded_rows(pad, block):
    pad[:CIN, :] = block
    return pad[...]


def store_weight(weight, t, block):
    a, b = t // 3, t % 3
    hi, lo = split(block)
    weight[a, b * LANES : (b + 1) * LANES, :LANES] = hi
    weight[a, b * LANES : (b + 1) * LANES, LANES:] = lo


def prepare_kernel(own, north, south, w_first, w_second, x, w1, w2, pad):
    x[...] = jnp.zeros_like(x)
    for i in range(ROWS + 8):
        r = i * PITCH
        row = north[i] if i < 4 else own[i - 4] if i < ROWS + 4 else south[i - ROWS - 4]
        x[r + 8 : r + 8 + COLS, :CIN] = row
    pad[...] = jnp.zeros_like(pad)
    for a in range(3):
        for b in range(3):
            pad[b * CIN : (b + 1) * CIN, :] = w_first[3 * a + b]
        hi, lo = split(pad[...])
        w1[a, :, :LANES] = hi
        w1[a, :, LANES:] = lo
    for t in range(9):
        store_weight(w2, t, w_second[t].T)


def forward_kernel(consts, centre, west, east, w1, w2, cells, a1, s1, s2, small, x, slopes, high, low, high1, low1):
    b1, b2 = consts[0:1, :], consts[1:2, :]
    weights = [consts[6:7, i : i + 1] for i in range(ROWS + 6)]
    x[...] = centre[...]
    for i in range(ROWS + 8):
        r = i * PITCH
        x[r + 4 : r + 8, :CIN] = west[i]
        x[r + 8 + COLS : r + 12 + COLS, :CIN] = east[i]
    cells[...] = x[3 * PITCH : 21 * PITCH + 8, :]
    spread_packed(x, high1, low1, 0, NX)
    for first, rows in chunks(ROWS + 6, 2):
        acc = convolve(high1, low1, w1, first * PITCH, rows * PITCH)
        for k in range(rows):
            r = (first + k) * PITCH
            h = acc[k * PITCH : (k + 1) * PITCH] + b1
            sigma = jax.nn.sigmoid(h)
            inside = jnp.where(weights[first + k] > 0.0, 1.0, 0.0)
            a1[r : r + PITCH, :] = h * sigma * inside
            slopes[r : r + PITCH, :] = sigma * (1.0 + h * (1.0 - sigma)) * inside
    a1[N1:, :] = jnp.zeros((8, LANES), F32)
    s1[...] = slopes[2 * PITCH + 2 : 2 * PITCH + 2 + N3, :]
    spread(a1, high, low, 0, N1)
    mask = column_mask(6, (PITCH, LANES))
    pooled = jnp.zeros((PITCH, LANES), F32)
    bias = jnp.zeros((PITCH, LANES), F32)
    for first, rows in chunks(ROWS + 4, 2):
        acc = convolve(high, low, w2, first * PITCH, rows * PITCH)
        for k in range(rows):
            i = first + k
            r = i * PITCH
            h = acc[k * PITCH : (k + 1) * PITCH] + b2
            sigma = jax.nn.sigmoid(h)
            weight = weights[i + 1]
            slope = sigma * (1.0 + h * (1.0 - sigma)) * weight
            s2[r : r + PITCH, :] = slope
            if 2 <= i < ROWS + 2:
                pooled = pooled + h * sigma * weight
                bias = bias + slope
    s2[N2:, :] = jnp.zeros((8, LANES), F32)
    small[0:1, :] = jnp.sum(pooled * mask, axis=0, keepdims=True)
    small[1:2, :] = jnp.sum(bias * mask, axis=0, keepdims=True)


def write_pieces(out, rows, extra=None):
    count, size = out.shape[0], out.shape[1] - (0 if extra is None else extra.shape[0])
    for p in range(count):
        q = (p % 2) * (count // 2) + p // 2
        out[p, :size] = rows[q * size : (q + 1) * size, :]
        if extra is not None:
            out[p, size:] = extra[...]


def second_kernel(a1, s2, small, out, high, low, rows):
    spread(a1, high, low, 2 * PITCH, 20 * PITCH)
    mask = column_mask(6, (PITCH, LANES))
    own = [s2[(i + 2) * PITCH : (i + 3) * PITCH, :] * mask for i in range(ROWS)]
    grad = jnp.concatenate(own + [jnp.zeros((PITCH, LANES), F32)], axis=0)
    for a, block in enumerate(correlate(grad, high, low, 2 * PITCH)):
        for b in range(3):
            t = 3 * a + b
            rows[t * LANES : (t + 1) * LANES, :] = block[:, b * LANES : (b + 1) * LANES]
    write_pieces(out, rows, small)


def mode_gradients(sums, modes, consts):
    total = jnp.sum(sums[...], axis=0)
    pooled = total[0:1]
    amplitude = jnp.sum(modes[...] * pooled, axis=1, keepdims=True)
    count = amplitude.shape[0]
    cotangent = jnp.concatenate(
        [jnp.broadcast_to(consts[k : k + 1, :], (LANES, LANES)).T[:, :1] for k in range(2, 2 + count // LANES)], axis=0
    )
    width = jnp.sqrt(jnp.sum(amplitude * amplitude, axis=0, keepdims=True) / count + 1e-05)
    normal = amplitude / width
    along = jnp.sum(cotangent * normal, axis=0, keepdims=True) / count
    d_amplitude = (cotangent - normal * along) / width
    d_pooled = jnp.sum(d_amplitude * modes[...], axis=0, keepdims=True)
    return total, pooled, d_amplitude, d_pooled


def share_kernel(parts, out):
    total = jnp.sum(parts[...], axis=0)
    bit, size = out.shape[1] - 2, total.shape[0] - 2
    for z in range(out.shape[0]):
        out[z] = jnp.zeros_like(out[z])
        out[z, :2] = total[size:]
        count = min(bit, size - z * bit)
        if count > 0:
            out[z, 2 : 2 + count] = total[z * bit : z * bit + count]


def ring_kernel(parts, sums, out):
    part = jnp.sum(parts[...], axis=0)
    bit = jnp.sum(sums[...], axis=0)[2:]
    for z in range(out.shape[0]):
        out[z, : part.shape[0]] = part
        out[z, part.shape[0] :] = bit


def plane_kernel(size, both, out, rows):
    first = out.shape[1] - size
    part = jnp.sum(both[...], axis=0)[:first]
    bit = both.shape[1] - first
    for z in range(-(-size // bit)):
        count = min(bit, size - z * bit)
        rows[z * bit : z * bit + count, :] = both[z, first : first + count]
    second = rows[...]
    for p in range(out.shape[0]):
        out[p, :size] = second
        out[p, size:] = part


def backward_kernel(sums, modes, consts, s1, s2, x, w_second, out, g1, weight, rows, high, low, high1, low1):
    spread(s2, high, low, 0, N2)
    d_pooled = mode_gradients(sums, modes, consts)[3]
    column = jnp.broadcast_to(d_pooled, (LANES, LANES)).T
    for t in range(9):
        store_weight(weight, t, w_second[8 - t] * column)
    for first, count in chunks(ROWS + 2, 6):
        r, n = first * PITCH, count * PITCH
        g1[r : r + n, :] = convolve(high, low, weight, r, n) * s1[r : r + n, :]
    g1[N3:, :] = jnp.zeros((8, LANES), F32)

    mask = column_mask(7, (PITCH, LANES))
    own = [g1[(i + 1) * PITCH - 2 : (i + 2) * PITCH - 2, :] * mask for i in range(ROWS)]
    bias1 = own[0]
    for row in own[1:]:
        bias1 = bias1 + row
    grad = jnp.concatenate(own + [jnp.zeros((PITCH, LANES), F32)], axis=0)
    spread_packed(x, high1, low1, 0, 18 * PITCH)
    for a, block in enumerate(correlate(grad, high1, low1, 0)):
        rows[3 * a * CIN : 3 * (a + 1) * CIN, :] = block.T[: 3 * CIN]
    rows[9 * CIN : 9 * CIN + 1, :] = jnp.sum(bias1, axis=0, keepdims=True)
    rows[9 * CIN + 1 :, :] = jnp.zeros((rows.shape[0] - 9 * CIN - 1, LANES), F32)
    write_pieces(out, rows)


def field_kernel(scale, g1, w_first, sums, modes, consts, out, d_modes, spread_d, bias2, weight, pad, high, low):
    total, pooled, d_amplitude, d_pooled = mode_gradients(sums, modes, consts)
    d_modes[...] = d_amplitude * pooled
    spread_d[...] = jnp.broadcast_to(d_pooled, (LANES, LANES)).T
    bias2[...] = total[1:2] * d_pooled
    pad[...] = jnp.zeros_like(pad)
    for t in range(9):
        store_weight(weight, t, padded_rows(pad, w_first[8 - t]).T)
    spread(g1, high, low, 0, N3)
    for first, count in chunks(ROWS, 2):
        acc = convolve(high, low, weight, first * PITCH, count * PITCH) * scale
        for k in range(count):
            out[first + k] = acc[k * PITCH + 4 : k * PITCH + 4 + COLS, :CIN]


def finish_kernel(core, mine, other, spread_d, w_second, w_first, b_first, rows):
    chips = mine.shape[0]
    size = 9 * LANES // (2 * chips)
    rest = mine.shape[1] - size
    even = core[0] == 0

    def gather(start, count):
        for p in range(chips):
            m, o = mine[p, start : start + count, :], other[p, start : start + count, :]
            rows[p * count : (p + 1) * count, :] = jnp.where(even, m, o)
            rows[(chips + p) * count : (chips + p + 1) * count, :] = jnp.where(even, o, m)

    gather(0, size)
    for t in range(9):
        w_second[t] = rows[t * LANES : (t + 1) * LANES, :] * spread_d[...]
    gather(size, rest)
    for t in range(9):
        w_first[t] = rows[t * CIN : (t + 1) * CIN, :]
    b_first[...] = rows[9 * CIN : 9 * CIN + 1, :]


def call(kernel, outs, scratch, flops, smem=()):
    outs = [o if isinstance(o[0], tuple) else (o, F32) for o in outs]

    def run(*args):
        return pl.pallas_call(
            kernel,
            out_shape=[jax.ShapeDtypeStruct(s, d) for s, d in outs],
            in_specs=[pl.BlockSpec(memory_space=pltpu.SMEM if i in smem else pltpu.VMEM) for i in range(len(args))],
            out_specs=[pl.BlockSpec(memory_space=pltpu.VMEM) for _ in outs],
            scratch_shapes=[pltpu.VMEM(s, d) for s, d in scratch],
            compiler_params=pltpu.CompilerParams(vmem_limit_bytes=12 << 20),
            cost_estimate=pl.CostEstimate(flops=flops, bytes_accessed=4 << 20, transcendentals=0),
        )(*args)

    return run


def edges(cells, axes, dim, width, closed):
    count = lax.axis_size(axes)
    ends = count if closed else count - 1
    head = lax.slice_in_dim(cells, 0, width, axis=dim)
    tail = lax.slice_in_dim(cells, cells.shape[dim] - width, cells.shape[dim], axis=dim)
    before = lax.ppermute(tail, axes, [(i, (i + 1) % count) for i in range(ends)])
    after = lax.ppermute(head, axes, [((i + 1) % count, i) for i in range(ends)])
    return before, after


def row_weights(first, count, nlat, nlon):
    phi = (np.arange(nlat) + 0.5) * (math.pi / nlat) - math.pi / 2
    table = np.zeros(nlat + 2 * count, np.float32)
    table[count : count + nlat] = np.cos(phi) / (np.cos(phi).sum() * nlon)
    return lax.dynamic_slice(jnp.asarray(table), (first + count,), (count,))


def swap(pieces, axes):
    return lax.all_to_all(pieces, axes, 0, 0, tiled=True)


def body(field, w_first, b_first, w_second, b_second, modes, cotangent):
    cin, rows, cols = field.shape
    ch = w_first.shape[1]
    n_lat, n_lon = lax.axis_size(LAT), lax.axis_size(LON)
    n_pl, n_z = lax.axis_size(PLANE), lax.axis_size(RING)
    nlat, nlon = rows * n_lat, cols * n_lon
    weights = row_weights(lax.axis_index(LAT) * rows - 3, rows + 6, nlat, nlon)
    consts = jnp.concatenate([b_first, b_second, cotangent, weights, jnp.zeros(LANES - rows - 6, F32)]).reshape(-1, LANES)

    own = field.transpose(1, 2, 0)
    north, south = edges(own, LAT, 0, 4, False)
    left = jnp.concatenate([north[:, :4], own[:, :4], south[:, :4]], axis=0)
    right = jnp.concatenate([north[:, cols - 4 :], own[:, cols - 4 :], south[:, cols - 4 :]], axis=0)
    west, east = edges(jnp.concatenate([left, right], axis=1), LON, 1, 4, True)
    w_first = w_first.transpose(0, 2, 1)
    weight = ((3, 3 * LANES, 2 * LANES), BF16)
    packed = ((3, 2 * LANES, 2 * LANES), BF16)
    pad = ((LANES, LANES), F32)
    pair = lambda n, width=3 * LANES: [((n, width), BF16), ((n, width), BF16)]
    centre, w1, w2 = call(prepare_kernel, [(NX + 8, LANES), packed, weight], [((2 * LANES, LANES), F32)], 10**9)(
        own, north, south, w_first, w_second
    )
    x, a1, s1, s2, small = call(
        forward_kernel,
        [(18 * PITCH + 8, LANES), (N1 + 8, LANES), (N3, LANES), (N2 + 8, LANES), (2, LANES)],
        [((NX + 8, LANES), F32), ((N1, LANES), F32)] + pair(N1) + pair(NX, 2 * LANES),
        10**9,
    )(consts, centre, west, east, w1, w2)

    share2 = 9 * ch // n_pl
    (part,) = call(second_kernel, [(n_pl, share2 + 2, ch)], pair(20 * PITCH) + [((9 * ch, LANES), F32)], 10**9)(a1, s2, small)

    bit2 = -(-share2 // n_z)
    (mine,) = call(share_kernel, [(n_z, bit2 + 2, ch)], [], 10**6)(swap(part, PLANE))
    mine = swap(mine, RING)

    share1 = -(-(9 * cin + 1) // n_pl)
    g1rows, g1 = call(
        backward_kernel,
        [(n_pl, share1, ch), (N3 + 8, LANES)],
        [weight, ((n_pl * share1, LANES), F32)] + pair(N2) + pair(18 * PITCH, 2 * LANES),
        10**9,
    )(mine, modes, consts, s1, s2, x, w_second)

    part = swap(g1rows, PLANE)
    grad_field, d_modes, spread_d, bias2 = call(
        lambda *r: field_kernel(float(nlat * nlon), *r),
        [(rows, cols, cin), modes.shape, (LANES, LANES), (1, LANES)],
        [weight, pad] + pair(N3),
        10**9,
    )(g1, w_first, mine, modes, consts)
    part, grad_field = lax.optimization_barrier((part, grad_field))
    (both,) = call(ring_kernel, [(n_z, share1 + bit2, ch)], [], 10**6)(part, mine)
    (whole,) = call(
        lambda *r: plane_kernel(share2, *r), [(n_pl // 2, share2 + share1, ch)], [((share2, LANES), F32)], 10**6
    )(swap(both, RING))
    whole = swap(whole, CHIPS)
    other = lax.ppermute(whole, "c", [(0, 1), (1, 0)])
    core = lax.axis_index("c").astype(jnp.int32).reshape(1)
    grad_w_second, grad_w_first, grad_b_first = call(
        finish_kernel,
        [(9, ch, ch), (9, cin, ch), (1, ch)],
        [((9 * ch, LANES), F32)],
        10**6,
        (0,),
    )(core, whole, other, spread_d)
    return (grad_field.transpose(2, 0, 1), grad_w_first.transpose(0, 2, 1), grad_b_first[0], grad_w_second, bias2[0], d_modes)


def solution(mesh):
    fine = Mesh(mesh.devices.reshape(4, 2, 2, 16, 2), ("y", "xl", "c", "z", "xh"))
    in_specs = (P(None, LAT, LON), P(), P(), P(), P(), P(), P())
    out_specs = (P(None, LAT, LON), P(), P(), P(), P(), P())
    return jax.shard_map(body, mesh=fine, in_specs=in_specs, out_specs=out_specs, check_vma=False)
```

```python
import math

import jax
import jax.numpy as jnp
import numpy as np
from jax import lax
from jax.experimental import pallas as pl
from jax.experimental.pallas import tpu as pltpu
from jax.sharding import Mesh, PartitionSpec as P

LAT = ("y", "xl", "c")
LON = ("z", "xh")
CHIPS = ("y", "xl", "xh")
PLANE = ("y", "xl", "xh", "c")
RING = ("z",)
F32 = jnp.float32
BF16 = jnp.bfloat16

PITCH = 64
LANES = 128
ROWS, COLS, CIN = 15, 45, 69
WINDOW = 16 * PITCH
NX, N1, N2, N3 = 23 * PITCH, 21 * PITCH, 19 * PITCH, 17 * PITCH


def split(x):
    hi = x.astype(BF16)
    return hi, (x - hi.astype(F32)).astype(BF16)


def spread(src, high, low, start, stop):
    for r in range(start, stop, PITCH):
        for b in range(3):
            hi, lo = split(src[r + b : r + b + PITCH, :])
            high[r : r + PITCH, b * LANES : (b + 1) * LANES] = hi
            low[r : r + PITCH, b * LANES : (b + 1) * LANES] = lo


def spread_packed(src, high, low, start, stop):
    lane = lax.broadcasted_iota(jnp.int32, (PITCH, LANES), 1)
    for r in range(start, stop, PITCH):
        second = pltpu.roll(src[r + 1 : r + 1 + PITCH, :], CIN, 1)
        third = pltpu.roll(src[r + 2 : r + 2 + PITCH, :], 2 * CIN - LANES, 1)
        for k, x in enumerate(
            (jnp.where(lane < CIN, src[r : r + PITCH, :], second), jnp.where(lane < 2 * CIN - LANES, second, third))
        ):
            hi, lo = split(x)
            high[r : r + PITCH, k * LANES : (k + 1) * LANES] = hi
            low[r : r + PITCH, k * LANES : (k + 1) * LANES] = lo


def dot(a, b):
    return jnp.dot(a, b, preferred_element_type=F32)


def convolve(high, low, weight, start, count):
    def taps(src):
        return jnp.concatenate([src[start + a * PITCH : start + a * PITCH + count, :] for a in range(3)], axis=1)

    w = jnp.concatenate([weight[a] for a in range(3)], axis=0)
    both = dot(taps(high), w)
    return both[:, :LANES] + both[:, LANES:] + dot(taps(low), w[:, :LANES])


def correlate(grad, high, low, start, spans):
    hi, lo = split(grad.T)
    both = jnp.concatenate([hi, lo], axis=0)
    blocks = []
    for a, first, last in spans:
        r = slice(start + a * PITCH, start + a * PITCH + WINDOW)
        out = dot(both, high[r, first:last])
        blocks.append(out[:LANES] + out[LANES:] + dot(hi, low[r, first:last]))
    return blocks


HALVES = (((0, 0, 3 * LANES), (1, 0, 2 * LANES)), ((1, LANES, 3 * LANES), (2, 0, 3 * LANES)))
HALF = 9 * LANES // 2


def correlate_half(core, s2, high, low, start, out):
    mask = column_mask(6, (PITCH, LANES))
    own = [s2[(i + 2) * PITCH : (i + 3) * PITCH, :] * mask for i in range(ROWS)]
    grad = jnp.concatenate(own + [jnp.zeros((PITCH, LANES), F32)], axis=0)
    for half in range(2):

        @pl.when(core == half)
        def _():
            r = -half * (LANES // 2)
            for block in correlate(grad, high, low, start, HALVES[half]):
                for k in range(0, block.shape[1], LANES):
                    first, last = max(r, 0), min(r + LANES, HALF)
                    out[first:last, :] = block[first - r : last - r, k : k + LANES]
                    r += LANES


def chunks(rows, parts):
    size = -(-rows // parts)
    return [(s, min(size, rows - s)) for s in range(0, rows, size)]


def column_mask(first, shape):
    col = lax.broadcasted_iota(jnp.int32, shape, 0)
    return ((col >= first) & (col < first + COLS)).astype(F32)


def padded_rows(pad, block):
    pad[:CIN, :] = block
    return pad[...]


def store_weight(weight, t, block):
    a, b = t // 3, t % 3
    hi, lo = split(block)
    weight[a, b * LANES : (b + 1) * LANES, :LANES] = hi
    weight[a, b * LANES : (b + 1) * LANES, LANES:] = lo


def prepare_kernel(core, own, inner, outer, w_first, w_second, x, w1, w2, pad):
    first = core[0] == 0
    x[...] = jnp.zeros_like(x)
    for i in range(ROWS + 8):
        r = i * PITCH
        if i < 4:
            row = jnp.where(first, outer[i], inner[i])
        elif i < ROWS + 4:
            row = own[i - 4]
        else:
            row = jnp.where(first, inner[i - ROWS - 4], outer[i - ROWS - 4])
        x[r + 8 : r + 8 + COLS, :CIN] = row
    pad[...] = jnp.zeros_like(pad)
    for a in range(3):
        for b in range(3):
            pad[b * CIN : (b + 1) * CIN, :] = w_first[3 * a + b]
        hi, lo = split(pad[...])
        w1[a, :, :LANES] = hi
        w1[a, :, LANES:] = lo
    for t in range(9):
        store_weight(w2, t, w_second[t].T)


def forward_kernel(core, half, consts, centre, outer, inner, w1, w2, cells, a1, s1, s2, small, send, x, slopes, high, low, high1, low1):
    first = half[0] == 0
    b1, b2 = consts[0:1, :], consts[1:2, :]
    weights = [consts[6:7, i : i + 1] for i in range(ROWS + 6)]
    x[...] = centre[...]
    for i in range(ROWS + 8):
        r = i * PITCH
        x[r + 4 : r + 8, :CIN] = jnp.where(first, outer[i], inner[i])
        x[r + 8 + COLS : r + 12 + COLS, :CIN] = jnp.where(first, inner[i], outer[i])
    cells[...] = x[3 * PITCH : 21 * PITCH + 8, :]
    spread_packed(x, high1, low1, 0, NX)
    for first, rows in chunks(ROWS + 6, 2):
        acc = convolve(high1, low1, w1, first * PITCH, rows * PITCH)
        for k in range(rows):
            r = (first + k) * PITCH
            h = acc[k * PITCH : (k + 1) * PITCH] + b1
            sigma = jax.nn.sigmoid(h)
            inside = jnp.where(weights[first + k] > 0.0, 1.0, 0.0)
            a1[r : r + PITCH, :] = h * sigma * inside
            slopes[r : r + PITCH, :] = sigma * (1.0 + h * (1.0 - sigma)) * inside
    a1[N1:, :] = jnp.zeros((8, LANES), F32)
    s1[...] = slopes[2 * PITCH + 2 : 2 * PITCH + 2 + N3, :]
    spread(a1, high, low, 0, N1)
    mask = column_mask(6, (PITCH, LANES))
    pooled = jnp.zeros((PITCH, LANES), F32)
    bias = jnp.zeros((PITCH, LANES), F32)
    for first, rows in chunks(ROWS + 4, 2):
        acc = convolve(high, low, w2, first * PITCH, rows * PITCH)
        for k in range(rows):
            i = first + k
            r = i * PITCH
            h = acc[k * PITCH : (k + 1) * PITCH] + b2
            sigma = jax.nn.sigmoid(h)
            weight = weights[i + 1]
            slope = sigma * (1.0 + h * (1.0 - sigma)) * weight
            s2[r : r + PITCH, :] = slope
            if 2 <= i < ROWS + 2:
                pooled = pooled + h * sigma * weight
                bias = bias + slope
    s2[N2:, :] = jnp.zeros((8, LANES), F32)
    small[0:1, :] = jnp.sum(pooled * mask, axis=0, keepdims=True)
    small[1:2, :] = jnp.sum(bias * mask, axis=0, keepdims=True)
    correlate_half(1 - core[0], s2, high, low, 2 * PITCH, send)
    send[HALF : HALF + 2, :] = small[...]


def write_pieces(out, rows):
    count, size = out.shape[0], out.shape[1]
    for p in range(count):
        q = (p % 2) * (count // 2) + p // 2
        out[p] = rows[q * size : (q + 1) * size, :]


def second_kernel(core, a1, s2, out, high, low):
    spread(a1.at[2 * PITCH :], high, low, 0, 18 * PITCH)
    correlate_half(core[0], s2, high, low, 0, out)


def pair_kernel(own, other, small, out):
    size = out.shape[1] - 2
    sums = small[...] + other[HALF : HALF + 2, :]
    for p in range(out.shape[0]):
        r = slice(p * size, (p + 1) * size)
        out[p, :size] = own[r, :] + other[r, :]
        out[p, size:] = sums


def mode_gradients(sums, modes, consts):
    total = jnp.sum(sums[...], axis=0)
    pooled = total[0:1]
    amplitude = jnp.sum(modes[...] * pooled, axis=1, keepdims=True)
    count = amplitude.shape[0]
    cotangent = jnp.concatenate(
        [jnp.broadcast_to(consts[k : k + 1, :], (LANES, LANES)).T[:, :1] for k in range(2, 2 + count // LANES)], axis=0
    )
    width = jnp.sqrt(jnp.sum(amplitude * amplitude, axis=0, keepdims=True) / count + 1e-05)
    normal = amplitude / width
    along = jnp.sum(cotangent * normal, axis=0, keepdims=True) / count
    d_amplitude = (cotangent - normal * along) / width
    d_pooled = jnp.sum(d_amplitude * modes[...], axis=0, keepdims=True)
    return total, pooled, d_amplitude, d_pooled


def share_kernel(parts, out):
    total = jnp.sum(parts[...], axis=0)
    bit, size = out.shape[1] - 2, total.shape[0] - 2
    for z in range(out.shape[0]):
        out[z] = jnp.zeros_like(out[z])
        out[z, :2] = total[size:]
        count = min(bit, size - z * bit)
        if count > 0:
            out[z, 2 : 2 + count] = total[z * bit : z * bit + count]


def ring_kernel(parts, sums, out):
    part = jnp.sum(parts[...], axis=0)
    bit = jnp.sum(sums[...], axis=0)[2:]
    for z in range(out.shape[0]):
        out[z, : part.shape[0]] = part
        out[z, part.shape[0] :] = bit


def plane_kernel(size, both, out, rows):
    first = out.shape[1] - size
    part = jnp.sum(both[...], axis=0)[:first]
    bit = both.shape[1] - first
    for z in range(-(-size // bit)):
        count = min(bit, size - z * bit)
        rows[z * bit : z * bit + count, :] = both[z, first : first + count]
    second = rows[...]
    for p in range(out.shape[0]):
        out[p, :size] = second
        out[p, size:] = part


def backward_kernel(sums, modes, consts, s1, s2, x, w_second, out, g1, weight, rows, high, low, high1, low1):
    spread(s2, high, low, 0, N2)
    d_pooled = mode_gradients(sums, modes, consts)[3]
    column = jnp.broadcast_to(d_pooled, (LANES, LANES)).T
    for t in range(9):
        store_weight(weight, t, w_second[8 - t] * column)
    for first, count in chunks(ROWS + 2, 6):
        r, n = first * PITCH, count * PITCH
        g1[r : r + n, :] = convolve(high, low, weight, r, n) * s1[r : r + n, :]
    g1[N3:, :] = jnp.zeros((8, LANES), F32)

    mask = column_mask(7, (PITCH, LANES))
    own = [g1[(i + 1) * PITCH - 2 : (i + 2) * PITCH - 2, :] * mask for i in range(ROWS)]
    bias1 = own[0]
    for row in own[1:]:
        bias1 = bias1 + row
    grad = jnp.concatenate(own + [jnp.zeros((PITCH, LANES), F32)], axis=0)
    spread_packed(x, high1, low1, 0, 18 * PITCH)
    for a, block in enumerate(correlate(grad, high1, low1, 0, [(a, 0, 2 * LANES) for a in range(3)])):
        rows[3 * a * CIN : 3 * (a + 1) * CIN, :] = block.T[: 3 * CIN]
    rows[9 * CIN : 9 * CIN + 1, :] = jnp.sum(bias1, axis=0, keepdims=True)
    rows[9 * CIN + 1 :, :] = jnp.zeros((rows.shape[0] - 9 * CIN - 1, LANES), F32)
    write_pieces(out, rows)


def field_kernel(scale, g1, w_first, sums, modes, consts, out, d_modes, spread_d, bias2, weight, pad, high, low):
    total, pooled, d_amplitude, d_pooled = mode_gradients(sums, modes, consts)
    d_modes[...] = d_amplitude * pooled
    spread_d[...] = jnp.broadcast_to(d_pooled, (LANES, LANES)).T
    bias2[...] = total[1:2] * d_pooled
    pad[...] = jnp.zeros_like(pad)
    for t in range(9):
        store_weight(weight, t, padded_rows(pad, w_first[8 - t]).T)
    spread(g1, high, low, 0, N3)
    for first, count in chunks(ROWS, 2):
        acc = convolve(high, low, weight, first * PITCH, count * PITCH) * scale
        for k in range(count):
            out[first + k] = acc[k * PITCH + 4 : k * PITCH + 4 + COLS, :CIN]


def finish_kernel(core, mine, other, spread_d, w_second, w_first, b_first, rows):
    chips = mine.shape[0]
    size = HALF // chips
    rest = mine.shape[1] - size
    even = core[0] == 0

    def gather(start, count):
        for p in range(chips):
            m, o = mine[p, start : start + count, :], other[p, start : start + count, :]
            rows[p * count : (p + 1) * count, :] = jnp.where(even, m, o)
            rows[(chips + p) * count : (chips + p + 1) * count, :] = jnp.where(even, o, m)

    gather(0, size)
    for t in range(9):
        w_second[t] = rows[t * LANES : (t + 1) * LANES, :] * spread_d[...]
    gather(size, rest)
    for t in range(9):
        w_first[t] = rows[t * CIN : (t + 1) * CIN, :]
    b_first[...] = rows[9 * CIN : 9 * CIN + 1, :]


def call(kernel, outs, scratch, flops, smem=()):
    outs = [o if isinstance(o[0], tuple) else (o, F32) for o in outs]

    def run(*args):
        return pl.pallas_call(
            kernel,
            out_shape=[jax.ShapeDtypeStruct(s, d) for s, d in outs],
            in_specs=[pl.BlockSpec(memory_space=pltpu.SMEM if i in smem else pltpu.VMEM) for i in range(len(args))],
            out_specs=[pl.BlockSpec(memory_space=pltpu.VMEM) for _ in outs],
            scratch_shapes=[pltpu.VMEM(s, d) for s, d in scratch],
            compiler_params=pltpu.CompilerParams(vmem_limit_bytes=12 << 20),
            cost_estimate=pl.CostEstimate(flops=flops, bytes_accessed=4 << 20, transcendentals=0),
        )(*args)

    return run


def far_pairs(count, closed):
    pairs = [(i, (i + 1) % count) for i in range(1, count if closed else count - 1, 2)]
    return pairs + [(j, i) for i, j in pairs]


def near_pairs(count):
    pairs = [(i, i + 1) for i in range(0, count, 2)]
    return pairs + [(j, i) for i, j in pairs]


def row_weights(first, count, nlat, nlon):
    phi = (np.arange(nlat) + 0.5) * (math.pi / nlat) - math.pi / 2
    table = np.zeros(nlat + 2 * count, np.float32)
    table[count : count + nlat] = np.cos(phi) / (np.cos(phi).sum() * nlon)
    return lax.dynamic_slice(jnp.asarray(table), (first + count,), (count,))


def swap(pieces, axes):
    return lax.all_to_all(pieces, axes, 0, 0, tiled=True)


def body(field, w_first, b_first, w_second, b_second, modes, cotangent):
    cin, rows, cols = field.shape
    ch = w_first.shape[1]
    n_lat, n_lon = lax.axis_size(LAT), lax.axis_size(LON)
    n_pl, n_z = lax.axis_size(PLANE), lax.axis_size(RING)
    nlat, nlon = rows * n_lat, cols * n_lon
    weights = row_weights(lax.axis_index(LAT) * rows - 3, rows + 6, nlat, nlon)
    consts = jnp.concatenate([b_first, b_second, cotangent, weights, jnp.zeros(LANES - rows - 6, F32)]).reshape(-1, LANES)

    own = field.transpose(1, 2, 0)
    core, half = lax.axis_index("c"), lax.axis_index("xh")
    inner = lax.ppermute(lax.dynamic_slice_in_dim(own, (1 - core) * (rows - 4), 4, 0), LAT, near_pairs(n_lat))
    outer = lax.ppermute(lax.dynamic_slice_in_dim(own, core * (rows - 4), 4, 0), LAT, far_pairs(n_lat, False))
    strips = []
    for start in (half * (cols - 4), (1 - half) * (cols - 4)):
        a, b, c = [lax.dynamic_slice_in_dim(v, start, 4, 1) for v in (outer, own, inner)]
        strips.append(jnp.concatenate([jnp.where(core == 0, a, c), b, jnp.where(core == 0, c, a)], axis=0))
    outer_strip = lax.ppermute(strips[0], LON, far_pairs(n_lon, True))
    inner_strip = lax.ppermute(strips[1], LON, near_pairs(n_lon))
    core, half = core.astype(jnp.int32).reshape(1), half.astype(jnp.int32).reshape(1)
    w_first = w_first.transpose(0, 2, 1)
    weight = ((3, 3 * LANES, 2 * LANES), BF16)
    packed = ((3, 2 * LANES, 2 * LANES), BF16)
    pad = ((LANES, LANES), F32)
    pair = lambda n, width=3 * LANES: [((n, width), BF16), ((n, width), BF16)]
    centre, w1, w2 = call(prepare_kernel, [(NX + 8, LANES), packed, weight], [((2 * LANES, LANES), F32)], 10**9, smem=(0,))(
        core, own, inner, outer, w_first, w_second
    )
    swap_cores = lambda v: lax.ppermute(v, "c", [(0, 1), (1, 0)])
    x, a1, s1, s2, small, send = call(
        forward_kernel,
        [(18 * PITCH + 8, LANES), (N1 + 8, LANES), (N3, LANES), (N2 + 8, LANES), (2, LANES), (HALF + 8, LANES)],
        [((NX + 8, LANES), F32), ((N1, LANES), F32)] + pair(N1) + pair(NX, 2 * LANES),
        10**9,
        smem=(0, 1),
    )(core, half, consts, centre, outer_strip, inner_strip, w1, w2)

    other = swap_cores(send)
    (half,) = call(second_kernel, [(HALF, LANES)], pair(18 * PITCH), 10**9, smem=(0,))(core, a1, s2)
    share2 = HALF * 2 // n_pl
    (part,) = call(pair_kernel, [(n_pl // 2, share2 + 2, ch)], [], 10**6)(half, other, small)
    bit2 = -(-share2 // n_z)
    (mine,) = call(share_kernel, [(n_z, bit2 + 2, ch)], [], 10**6)(swap(part, CHIPS))
    mine = swap(mine, RING)

    share1 = -(-(9 * cin + 1) // n_pl)
    g1rows, g1 = call(
        backward_kernel,
        [(n_pl, share1, ch), (N3 + 8, LANES)],
        [weight, ((n_pl * share1, LANES), F32)] + pair(N2) + pair(18 * PITCH, 2 * LANES),
        10**9,
    )(mine, modes, consts, s1, s2, x, w_second)

    part = swap(g1rows, PLANE)
    grad_field, d_modes, spread_d, bias2 = call(
        lambda *r: field_kernel(float(nlat * nlon), *r),
        [(rows, cols, cin), modes.shape, (LANES, LANES), (1, LANES)],
        [weight, pad] + pair(N3),
        10**9,
    )(g1, w_first, mine, modes, consts)
    part, grad_field = lax.optimization_barrier((part, grad_field))
    (both,) = call(ring_kernel, [(n_z, share1 + bit2, ch)], [], 10**6)(part, mine)
    (whole,) = call(
        lambda *r: plane_kernel(share2, *r), [(n_pl // 2, share2 + share1, ch)], [((share2, LANES), F32)], 10**6
    )(swap(both, RING))
    whole = swap(whole, CHIPS)
    other = swap_cores(whole)
    grad_w_second, grad_w_first, grad_b_first = call(
        finish_kernel,
        [(9, ch, ch), (9, cin, ch), (1, ch)],
        [((2 * HALF, LANES), F32)],
        10**6,
        (0,),
    )(core, whole, other, spread_d)
    return (grad_field.transpose(2, 0, 1), grad_w_first.transpose(0, 2, 1), grad_b_first[0], grad_w_second, bias2[0], d_modes)


def solution(mesh):
    fine = Mesh(mesh.devices.reshape(4, 2, 2, 16, 2), ("y", "xl", "c", "z", "xh"))
    in_specs = (P(None, LAT, LON), P(), P(), P(), P(), P(), P())
    out_specs = (P(None, LAT, LON), P(), P(), P(), P(), P())
    return jax.shard_map(body, mesh=fine, in_specs=in_specs, out_specs=out_specs, check_vma=False)
```

```python
import math

import jax
import jax.numpy as jnp
import numpy as np
from jax import lax
from jax.experimental import pallas as pl
from jax.experimental.pallas import tpu as pltpu
from jax.sharding import Mesh, PartitionSpec as P

LAT = ("y", "xl", "c")
LON = ("z", "xh")
CHIPS = ("y", "xl", "xh")
PLANE = ("y", "xl", "xh", "c")
RING = ("z",)
F32 = jnp.float32
BF16 = jnp.bfloat16

PITCH = 64
LANES = 128
ROWS, COLS, CIN = 15, 45, 69
SHORT = 48
NARROW = 16
WINDOW = 16 * SHORT
NX, N1, N2, N3 = 23 * PITCH, 21 * PITCH, 19 * PITCH, 17 * SHORT


def split(x):
    hi = x.astype(BF16)
    return hi, (x - hi.astype(F32)).astype(BF16)


def spread(src, high, low, rows, first=0, col=0, width=PITCH, pitch=PITCH):
    for i in range(rows):
        for b in range(3):
            r = (first + i) * pitch + col + b
            hi, lo = split(src[r : r + width, :])
            high[i * width : (i + 1) * width, b * LANES : (b + 1) * LANES] = hi
            low[i * width : (i + 1) * width, b * LANES : (b + 1) * LANES] = lo


def spread_packed(src, high, low, rows, col=0, width=PITCH, pitch=PITCH):
    lane = lax.broadcasted_iota(jnp.int32, (width, LANES), 1)
    for i in range(rows):
        r = i * pitch + col
        second = pltpu.roll(src[r + 1 : r + 1 + width, :], CIN, 1)
        third = pltpu.roll(src[r + 2 : r + 2 + width, :], 2 * CIN - LANES, 1)
        for k, x in enumerate(
            (jnp.where(lane < CIN, src[r : r + width, :], second), jnp.where(lane < 2 * CIN - LANES, second, third))
        ):
            hi, lo = split(x)
            high[i * width : (i + 1) * width, k * LANES : (k + 1) * LANES] = hi
            low[i * width : (i + 1) * width, k * LANES : (k + 1) * LANES] = lo


def dot(a, b):
    return jnp.dot(a, b, preferred_element_type=F32)


def convolve(high, low, weight, first, rows, pitch=PITCH):
    def taps(src):
        return jnp.concatenate([src[(first + a) * pitch : (first + a + rows) * pitch, :] for a in range(3)], axis=1)

    w = jnp.concatenate([weight[a] for a in range(3)], axis=0)
    both = dot(taps(high), w)
    return both[:, :LANES] + both[:, LANES:] + dot(taps(low), w[:, :LANES])


def correlate(grad, high, low, spans):
    hi, lo = split(grad.T)
    both = jnp.concatenate([hi, lo], axis=0)
    blocks = []
    for a, first, last in spans:
        r = slice(a * SHORT, a * SHORT + WINDOW)
        out = dot(both, high[r, first:last])
        blocks.append(out[:LANES] + out[LANES:] + dot(hi, low[r, first:last]))
    return blocks


HALVES = (((0, 0, 3 * LANES), (1, 0, 2 * LANES)), ((1, LANES, 3 * LANES), (2, 0, 3 * LANES)))
HALF = 9 * LANES // 2


def correlate_half(core, a1, s2, high, low, out):
    spread(a1, high, low, 18, first=2, col=6, width=SHORT)
    mask = column_mask(0, (SHORT, LANES))
    own = [s2[(i + 2) * PITCH + 6 : (i + 2) * PITCH + 6 + SHORT, :] * mask for i in range(ROWS)]
    grad = jnp.concatenate(own + [jnp.zeros((SHORT, LANES), F32)], axis=0)
    for half in range(2):

        @pl.when(core == half)
        def _():
            r = -half * (LANES // 2)
            for block in correlate(grad, high, low, HALVES[half]):
                for k in range(0, block.shape[1], LANES):
                    first, last = max(r, 0), min(r + LANES, HALF)
                    out[first:last, :] = block[first - r : last - r, k : k + LANES]
                    r += LANES


def chunks(rows, parts):
    size = -(-rows // parts)
    return [(s, min(size, rows - s)) for s in range(0, rows, size)]


def column_mask(first, shape):
    col = lax.broadcasted_iota(jnp.int32, shape, 0)
    return ((col >= first) & (col < first + COLS)).astype(F32)


def padded_rows(pad, block):
    pad[:CIN, :] = block
    return pad[...]


def store_weight(weight, t, block):
    a, b = t // 3, t % 3
    hi, lo = split(block)
    weight[a, b * LANES : (b + 1) * LANES, :LANES] = hi
    weight[a, b * LANES : (b + 1) * LANES, LANES:] = lo


def activate(h, inside):
    sigma = jax.nn.sigmoid(h)
    return h * sigma * inside, sigma * (1.0 + h * (1.0 - sigma)) * inside


def prepare_kernel(core, consts, own, inner, outer, w_first, w_second, x, a1, slopes, w1, w2, pad, high, low):
    upper = core[0] == 0
    x[...] = jnp.zeros_like(x)
    for i in range(ROWS + 8):
        r = i * PITCH
        if i < 4:
            row = jnp.where(upper, outer[i], inner[i])
        elif i < ROWS + 4:
            row = own[i - 4]
        else:
            row = jnp.where(upper, inner[i - ROWS - 4], outer[i - ROWS - 4])
        x[r + 8 : r + 8 + COLS, :CIN] = row
    pad[...] = jnp.zeros_like(pad)
    for a in range(3):
        for b in range(3):
            pad[b * CIN : (b + 1) * CIN, :] = w_first[3 * a + b]
        hi, lo = split(pad[...])
        w1[a, :, :LANES] = hi
        w1[a, :, LANES:] = lo
    spread_packed(x, high, low, ROWS + 8)
    for first, rows in chunks(ROWS + 6, 2):
        acc = convolve(high, low, w1, first, rows)
        for k in range(rows):
            i = first + k
            inside = jnp.where(consts[6:7, i : i + 1] > 0.0, 1.0, 0.0)
            r = slice(i * PITCH, (i + 1) * PITCH)
            a1[r, :], slopes[r, :] = activate(acc[k * PITCH : (k + 1) * PITCH] + consts[0:1, :], inside)
    a1[N1:, :] = jnp.zeros((8, LANES), F32)
    for t in range(9):
        store_weight(w2, t, w_second[t].T)


def forward_kernel(core, half, consts, centre, a1_part, slopes_part, outer, inner, w1, w2, cells, a1, s1, s2, small, send, x, slopes, edge, high, low, high1, low1, high2, low2):
    west = half[0] == 0
    b1, b2 = consts[0:1, :], consts[1:2, :]
    weights = [consts[6:7, i : i + 1] for i in range(ROWS + 6)]
    x[...] = centre[...]
    a1[...] = a1_part[...]
    slopes[...] = slopes_part[...]
    edge[...] = jnp.zeros_like(edge)
    for i in range(ROWS + 8):
        r, q = i * PITCH, i * NARROW
        x[r + 4 : r + 8, :CIN] = jnp.where(west, outer[i], inner[i])
        x[r + 8 + COLS : r + 12 + COLS, :CIN] = jnp.where(west, inner[i], outer[i])
        edge[q : q + 6, :] = x[r + 4 : r + 10, :]
        edge[q + 8 : q + 14, :] = x[r + 6 + COLS : r + 12 + COLS, :]
    cells[...] = x[3 * PITCH : 21 * PITCH + 8, :]
    spread_packed(edge, high1, low1, ROWS + 8, width=NARROW, pitch=NARROW)
    acc = convolve(high1, low1, w1, 0, ROWS + 6, NARROW)
    for i in range(ROWS + 6):
        r = i * PITCH
        inside = jnp.where(weights[i] > 0.0, 1.0, 0.0)
        active, slope = activate(acc[i * NARROW : (i + 1) * NARROW] + b1, inside)
        a1[r + 4 : r + 8, :] = active[:4]
        a1[r + 6 + COLS : r + 10 + COLS, :] = active[8:12]
        slopes[r + 4 : r + 8, :] = slope[:4]
        slopes[r + 6 + COLS : r + 10 + COLS, :] = slope[8:12]
    for i in range(ROWS + 2):
        r = (i + 2) * PITCH + 6
        s1[i * SHORT : (i + 1) * SHORT, :] = slopes[r : r + SHORT, :]
    spread(a1, high, low, ROWS + 6)
    mask = column_mask(6, (PITCH, LANES))
    pooled = jnp.zeros((PITCH, LANES), F32)
    bias = jnp.zeros((PITCH, LANES), F32)
    for first, rows in chunks(ROWS + 4, 2):
        acc = convolve(high, low, w2, first, rows)
        for k in range(rows):
            i = first + k
            r = i * PITCH
            h = acc[k * PITCH : (k + 1) * PITCH] + b2
            sigma = jax.nn.sigmoid(h)
            weight = weights[i + 1]
            slope = sigma * (1.0 + h * (1.0 - sigma)) * weight
            s2[r : r + PITCH, :] = slope
            if 2 <= i < ROWS + 2:
                pooled = pooled + h * sigma * weight
                bias = bias + slope
    s2[N2:, :] = jnp.zeros((8, LANES), F32)
    small[0:1, :] = jnp.sum(pooled * mask, axis=0, keepdims=True)
    small[1:2, :] = jnp.sum(bias * mask, axis=0, keepdims=True)
    correlate_half(1 - core[0], a1, s2, high2, low2, send)
    send[HALF : HALF + 2, :] = small[...]


def write_pieces(out, rows):
    count, size = out.shape[0], out.shape[1]
    for p in range(count):
        q = (p % 2) * (count // 2) + p // 2
        out[p] = rows[q * size : (q + 1) * size, :]


def second_kernel(core, a1, s2, out, high, low):
    correlate_half(core[0], a1, s2, high, low, out)


def pair_kernel(own, other, small, out):
    size = out.shape[1] - 2
    sums = small[...] + other[HALF : HALF + 2, :]
    for p in range(out.shape[0]):
        r = slice(p * size, (p + 1) * size)
        out[p, :size] = own[r, :] + other[r, :]
        out[p, size:] = sums


def mode_gradients(sums, modes, consts):
    total = jnp.sum(sums[...], axis=0)
    pooled = total[0:1]
    amplitude = jnp.sum(modes[...] * pooled, axis=1, keepdims=True)
    count = amplitude.shape[0]
    cotangent = jnp.concatenate(
        [jnp.broadcast_to(consts[k : k + 1, :], (LANES, LANES)).T[:, :1] for k in range(2, 2 + count // LANES)], axis=0
    )
    width = jnp.sqrt(jnp.sum(amplitude * amplitude, axis=0, keepdims=True) / count + 1e-05)
    normal = amplitude / width
    along = jnp.sum(cotangent * normal, axis=0, keepdims=True) / count
    d_amplitude = (cotangent - normal * along) / width
    d_pooled = jnp.sum(d_amplitude * modes[...], axis=0, keepdims=True)
    return total, pooled, d_amplitude, d_pooled


def share_kernel(parts, out):
    total = jnp.sum(parts[...], axis=0)
    bit, size = out.shape[1] - 2, total.shape[0] - 2
    for z in range(out.shape[0]):
        out[z] = jnp.zeros_like(out[z])
        out[z, :2] = total[size:]
        count = min(bit, size - z * bit)
        if count > 0:
            out[z, 2 : 2 + count] = total[z * bit : z * bit + count]


def ring_kernel(parts, sums, out):
    part = jnp.sum(parts[...], axis=0)
    bit = jnp.sum(sums[...], axis=0)[2:]
    for z in range(out.shape[0]):
        out[z, : part.shape[0]] = part
        out[z, part.shape[0] :] = bit


def plane_kernel(size, both, out, rows):
    first = out.shape[1] - size
    part = jnp.sum(both[...], axis=0)[:first]
    bit = both.shape[1] - first
    for z in range(-(-size // bit)):
        count = min(bit, size - z * bit)
        rows[z * bit : z * bit + count, :] = both[z, first : first + count]
    second = rows[...]
    for p in range(out.shape[0]):
        out[p, :size] = second
        out[p, size:] = part


def backward_kernel(sums, modes, consts, s1, s2, x, w_second, out, g1, weight, rows, high, low, high1, low1):
    spread(s2, high, low, ROWS + 4, col=4, width=SHORT)
    d_pooled = mode_gradients(sums, modes, consts)[3]
    column = jnp.broadcast_to(d_pooled, (LANES, LANES)).T
    for t in range(9):
        store_weight(weight, t, w_second[8 - t] * column)
    for first, count in chunks(ROWS + 2, 3):
        r = slice(first * SHORT, (first + count) * SHORT)
        g1[r, :] = convolve(high, low, weight, first, count, SHORT) * s1[r, :]
    g1[N3:, :] = jnp.zeros((8, LANES), F32)

    mask = column_mask(1, (SHORT, LANES))
    own = [g1[(i + 1) * SHORT : (i + 2) * SHORT, :] * mask for i in range(ROWS)]
    bias1 = own[0]
    for row in own[1:]:
        bias1 = bias1 + row
    grad = jnp.concatenate(own + [jnp.zeros((SHORT, LANES), F32)], axis=0)
    spread_packed(x, high1, low1, 18, col=6, width=SHORT)
    for a, block in enumerate(correlate(grad, high1, low1, [(a, 0, 2 * LANES) for a in range(3)])):
        rows[3 * a * CIN : 3 * (a + 1) * CIN, :] = block.T[: 3 * CIN]
    rows[9 * CIN : 9 * CIN + 1, :] = jnp.sum(bias1, axis=0, keepdims=True)
    rows[9 * CIN + 1 :, :] = jnp.zeros((rows.shape[0] - 9 * CIN - 1, LANES), F32)
    write_pieces(out, rows)


def field_kernel(scale, g1, w_first, sums, modes, consts, out, d_modes, spread_d, bias2, weight, pad, high, low):
    total, pooled, d_amplitude, d_pooled = mode_gradients(sums, modes, consts)
    d_modes[...] = d_amplitude * pooled
    spread_d[...] = jnp.broadcast_to(d_pooled, (LANES, LANES)).T
    bias2[...] = total[1:2] * d_pooled
    pad[...] = jnp.zeros_like(pad)
    for t in range(9):
        store_weight(weight, t, padded_rows(pad, w_first[8 - t]).T)
    spread(g1, high, low, ROWS + 2, width=SHORT, pitch=SHORT)
    for first, count in chunks(ROWS, 2):
        acc = convolve(high, low, weight, first, count, SHORT) * scale
        for k in range(count):
            out[first + k] = acc[k * SHORT : k * SHORT + COLS, :CIN]


def finish_kernel(core, mine, other, spread_d, w_second, w_first, b_first, rows):
    chips = mine.shape[0]
    size = HALF // chips
    rest = mine.shape[1] - size
    even = core[0] == 0

    def gather(start, count):
        for p in range(chips):
            m, o = mine[p, start : start + count, :], other[p, start : start + count, :]
            rows[p * count : (p + 1) * count, :] = jnp.where(even, m, o)
            rows[(chips + p) * count : (chips + p + 1) * count, :] = jnp.where(even, o, m)

    gather(0, size)
    for t in range(9):
        w_second[t] = rows[t * LANES : (t + 1) * LANES, :] * spread_d[...]
    gather(size, rest)
    for t in range(9):
        w_first[t] = rows[t * CIN : (t + 1) * CIN, :]
    b_first[...] = rows[9 * CIN : 9 * CIN + 1, :]


def call(kernel, outs, scratch, flops, smem=()):
    outs = [o if isinstance(o[0], tuple) else (o, F32) for o in outs]

    def run(*args):
        return pl.pallas_call(
            kernel,
            out_shape=[jax.ShapeDtypeStruct(s, d) for s, d in outs],
            in_specs=[pl.BlockSpec(memory_space=pltpu.SMEM if i in smem else pltpu.VMEM) for i in range(len(args))],
            out_specs=[pl.BlockSpec(memory_space=pltpu.VMEM) for _ in outs],
            scratch_shapes=[pltpu.VMEM(s, d) for s, d in scratch],
            compiler_params=pltpu.CompilerParams(vmem_limit_bytes=12 << 20),
            cost_estimate=pl.CostEstimate(flops=flops, bytes_accessed=4 << 20, transcendentals=0),
        )(*args)

    return run


def far_pairs(count, closed):
    pairs = [(i, (i + 1) % count) for i in range(1, count if closed else count - 1, 2)]
    return pairs + [(j, i) for i, j in pairs]


def near_pairs(count):
    pairs = [(i, i + 1) for i in range(0, count, 2)]
    return pairs + [(j, i) for i, j in pairs]


def row_weights(first, count, nlat, nlon):
    phi = (np.arange(nlat) + 0.5) * (math.pi / nlat) - math.pi / 2
    table = np.zeros(nlat + 2 * count, np.float32)
    table[count : count + nlat] = np.cos(phi) / (np.cos(phi).sum() * nlon)
    return lax.dynamic_slice(jnp.asarray(table), (first + count,), (count,))


def swap(pieces, axes):
    return lax.all_to_all(pieces, axes, 0, 0, tiled=True)


def body(field, w_first, b_first, w_second, b_second, modes, cotangent):
    cin, rows, cols = field.shape
    ch = w_first.shape[1]
    n_lat, n_lon = lax.axis_size(LAT), lax.axis_size(LON)
    n_pl, n_z = lax.axis_size(PLANE), lax.axis_size(RING)
    nlat, nlon = rows * n_lat, cols * n_lon
    weights = row_weights(lax.axis_index(LAT) * rows - 3, rows + 6, nlat, nlon)
    consts = jnp.concatenate([b_first, b_second, cotangent, weights, jnp.zeros(LANES - rows - 6, F32)]).reshape(-1, LANES)

    own = field.transpose(1, 2, 0)
    core, half = lax.axis_index("c"), lax.axis_index("xh")
    inner = lax.ppermute(lax.dynamic_slice_in_dim(own, (1 - core) * (rows - 4), 4, 0), LAT, near_pairs(n_lat))
    outer = lax.ppermute(lax.dynamic_slice_in_dim(own, core * (rows - 4), 4, 0), LAT, far_pairs(n_lat, False))
    strips = []
    for start in (half * (cols - 4), (1 - half) * (cols - 4)):
        a, b, c = [lax.dynamic_slice_in_dim(v, start, 4, 1) for v in (outer, own, inner)]
        strips.append(jnp.concatenate([jnp.where(core == 0, a, c), b, jnp.where(core == 0, c, a)], axis=0))
    outer_strip = lax.ppermute(strips[0], LON, far_pairs(n_lon, True))
    inner_strip = lax.ppermute(strips[1], LON, near_pairs(n_lon))
    core, half = core.astype(jnp.int32).reshape(1), half.astype(jnp.int32).reshape(1)
    w_first = w_first.transpose(0, 2, 1)
    weight = ((3, 3 * LANES, 2 * LANES), BF16)
    packed = ((3, 2 * LANES, 2 * LANES), BF16)
    pad = ((LANES, LANES), F32)
    pair = lambda n, width=3 * LANES: [((n, width), BF16), ((n, width), BF16)]
    centre, a1, slopes, w1, w2 = call(
        prepare_kernel,
        [(NX + 8, LANES), (N1 + 8, LANES), (N1, LANES), packed, weight],
        [((2 * LANES, LANES), F32)] + pair(NX, 2 * LANES),
        10**9,
        smem=(0,),
    )(core, consts, own, inner, outer, w_first, w_second)
    swap_cores = lambda v: lax.ppermute(v, "c", [(0, 1), (1, 0)])
    x, a1, s1, s2, small, send = call(
        forward_kernel,
        [(18 * PITCH + 8, LANES), (N1 + 8, LANES), (N3, LANES), (N2 + 8, LANES), (2, LANES), (HALF + 8, LANES)],
        [((NX + 8, LANES), F32), ((N1, LANES), F32), ((23 * NARROW + 8, LANES), F32)]
        + pair(N1)
        + pair(23 * NARROW, 2 * LANES)
        + pair(18 * SHORT),
        10**9,
        smem=(0, 1),
    )(core, half, consts, centre, a1, slopes, outer_strip, inner_strip, w1, w2)

    other = swap_cores(send)
    (half,) = call(second_kernel, [(HALF, LANES)], pair(18 * SHORT), 10**9, smem=(0,))(core, a1, s2)
    share2 = HALF * 2 // n_pl
    (part,) = call(pair_kernel, [(n_pl // 2, share2 + 2, ch)], [], 10**6)(half, other, small)
    bit2 = -(-share2 // n_z)
    (mine,) = call(share_kernel, [(n_z, bit2 + 2, ch)], [], 10**6)(swap(part, CHIPS))
    mine = swap(mine, RING)

    share1 = -(-(9 * cin + 1) // n_pl)
    g1rows, g1 = call(
        backward_kernel,
        [(n_pl, share1, ch), (N3 + 8, LANES)],
        [weight, ((n_pl * share1, LANES), F32)] + pair(19 * SHORT) + pair(18 * SHORT, 2 * LANES),
        10**9,
    )(mine, modes, consts, s1, s2, x, w_second)

    part = swap(g1rows, PLANE)
    grad_field, d_modes, spread_d, bias2 = call(
        lambda *r: field_kernel(float(nlat * nlon), *r),
        [(rows, cols, cin), modes.shape, (LANES, LANES), (1, LANES)],
        [weight, pad] + pair(N3),
        10**9,
    )(g1, w_first, mine, modes, consts)
    part, grad_field = lax.optimization_barrier((part, grad_field))
    (both,) = call(ring_kernel, [(n_z, share1 + bit2, ch)], [], 10**6)(part, mine)
    (whole,) = call(
        lambda *r: plane_kernel(share2, *r), [(n_pl // 2, share2 + share1, ch)], [((share2, LANES), F32)], 10**6
    )(swap(both, RING))
    whole = swap(whole, CHIPS)
    other = swap_cores(whole)
    grad_w_second, grad_w_first, grad_b_first = call(
        finish_kernel,
        [(9, ch, ch), (9, cin, ch), (1, ch)],
        [((2 * HALF, LANES), F32)],
        10**6,
        smem=(0,),
    )(core, whole, other, spread_d)
    return (grad_field.transpose(2, 0, 1), grad_w_first.transpose(0, 2, 1), grad_b_first[0], grad_w_second, bias2[0], d_modes)


def solution(mesh):
    fine = Mesh(mesh.devices.reshape(4, 2, 2, 16, 2), ("y", "xl", "c", "z", "xh"))
    in_specs = (P(None, LAT, LON), P(), P(), P(), P(), P(), P())
    out_specs = (P(None, LAT, LON), P(), P(), P(), P(), P())
    return jax.shard_map(body, mesh=fine, in_specs=in_specs, out_specs=out_specs, check_vma=False)
```

```python
import math

import jax
import jax.numpy as jnp
import numpy as np
from jax import lax
from jax.experimental import pallas as pl
from jax.experimental.pallas import tpu as pltpu
from jax.sharding import Mesh, PartitionSpec as P

LAT = ("y", "xl", "c")
LON = ("z", "xh")
CHIPS = ("y", "xl", "xh")
PLANE = ("y", "xl", "xh", "c")
RING = ("z",)
F32 = jnp.float32
BF16 = jnp.bfloat16

PITCH = 64
LANES = 128
ROWS, COLS, CIN = 15, 45, 69
SHORT = 48
NARROW = 16
WINDOW = 16 * SHORT
NX, N1, N2, N3 = 23 * PITCH, 21 * PITCH, 19 * PITCH, 17 * SHORT


def split(x):
    hi = x.astype(BF16)
    return hi, (x - hi.astype(F32)).astype(BF16)


def spread(src, high, low, rows, first=0, col=0, width=PITCH, pitch=PITCH):
    for i in range(rows):
        for b in range(3):
            r = (first + i) * pitch + col + b
            hi, lo = split(src[r : r + width, :])
            high[i * width : (i + 1) * width, b * LANES : (b + 1) * LANES] = hi
            low[i * width : (i + 1) * width, b * LANES : (b + 1) * LANES] = lo


def spread_packed(src, high, low, rows, col=0, width=PITCH, pitch=PITCH):
    lane = lax.broadcasted_iota(jnp.int32, (width, LANES), 1)
    for i in range(rows):
        r = i * pitch + col
        second = pltpu.roll(src[r + 1 : r + 1 + width, :], CIN, 1)
        third = pltpu.roll(src[r + 2 : r + 2 + width, :], 2 * CIN - LANES, 1)
        for k, x in enumerate(
            (jnp.where(lane < CIN, src[r : r + width, :], second), jnp.where(lane < 2 * CIN - LANES, second, third))
        ):
            hi, lo = split(x)
            high[i * width : (i + 1) * width, k * LANES : (k + 1) * LANES] = hi
            low[i * width : (i + 1) * width, k * LANES : (k + 1) * LANES] = lo


def dot(a, b):
    return jnp.dot(a, b, preferred_element_type=F32)


def convolve(high, low, weight, first, rows, pitch=PITCH):
    def taps(src):
        return jnp.concatenate([src[(first + a) * pitch : (first + a + rows) * pitch, :] for a in range(3)], axis=1)

    w = jnp.concatenate([weight[a] for a in range(3)], axis=0)
    both = dot(taps(high), w)
    return both[:, :LANES] + both[:, LANES:] + dot(taps(low), w[:, :LANES])


def correlate(grad, high, low, spans):
    hi, lo = split(grad.T)
    both = jnp.concatenate([hi, lo], axis=0)
    blocks = []
    for a, first, last in spans:
        r = slice(a * SHORT, a * SHORT + WINDOW)
        out = dot(both, high[r, first:last])
        blocks.append(out[:LANES] + out[LANES:] + dot(hi, low[r, first:last]))
    return blocks


HALVES = (((0, 0, 3 * LANES), (1, 0, 2 * LANES)), ((1, LANES, 3 * LANES), (2, 0, 3 * LANES)))
HALF = 9 * LANES // 2


def correlate_half(core, a1, s2, high, low, out):
    spread(a1, high, low, 18, first=2, col=6, width=SHORT)
    mask = column_mask(0, (SHORT, LANES))
    own = [s2[(i + 2) * PITCH + 6 : (i + 2) * PITCH + 6 + SHORT, :] * mask for i in range(ROWS)]
    grad = jnp.concatenate(own + [jnp.zeros((SHORT, LANES), F32)], axis=0)
    for half in range(2):

        @pl.when(core == half)
        def _():
            r = -half * (LANES // 2)
            for block in correlate(grad, high, low, HALVES[half]):
                for k in range(0, block.shape[1], LANES):
                    first, last = max(r, 0), min(r + LANES, HALF)
                    out[first:last, :] = block[first - r : last - r, k : k + LANES]
                    r += LANES


def chunks(rows, parts):
    size = -(-rows // parts)
    return [(s, min(size, rows - s)) for s in range(0, rows, size)]


def column_mask(first, shape):
    col = lax.broadcasted_iota(jnp.int32, shape, 0)
    return ((col >= first) & (col < first + COLS)).astype(F32)


def padded_rows(pad, block):
    pad[:CIN, :] = block
    return pad[...]


def store_weight(weight, t, block):
    a, b = t // 3, t % 3
    hi, lo = split(block)
    weight[a, b * LANES : (b + 1) * LANES, :LANES] = hi
    weight[a, b * LANES : (b + 1) * LANES, LANES:] = lo


def activate(h, inside):
    sigma = jax.nn.sigmoid(h)
    return h * sigma * inside, sigma * (1.0 + h * (1.0 - sigma)) * inside


def prepare_kernel(core, consts, own, inner, outer, w_first, w_second, x, a1, slopes, w1, w2, w1_back, pad, pad_back, high, low):
    upper = core[0] == 0
    x[...] = jnp.zeros_like(x)
    for i in range(ROWS + 8):
        r = i * PITCH
        if i < 4:
            row = jnp.where(upper, outer[i], inner[i])
        elif i < ROWS + 4:
            row = own[i - 4]
        else:
            row = jnp.where(upper, inner[i - ROWS - 4], outer[i - ROWS - 4])
        x[r + 8 : r + 8 + COLS, :CIN] = row
    pad[...] = jnp.zeros_like(pad)
    for a in range(3):
        for b in range(3):
            pad[b * CIN : (b + 1) * CIN, :] = w_first[3 * a + b]
        hi, lo = split(pad[...])
        w1[a, :, :LANES] = hi
        w1[a, :, LANES:] = lo
    spread_packed(x, high, low, ROWS + 8)
    for first, rows in chunks(ROWS + 6, 2):
        acc = convolve(high, low, w1, first, rows)
        for k in range(rows):
            i = first + k
            inside = jnp.where(consts[6:7, i : i + 1] > 0.0, 1.0, 0.0)
            r = slice(i * PITCH, (i + 1) * PITCH)
            a1[r, :], slopes[r, :] = activate(acc[k * PITCH : (k + 1) * PITCH] + consts[0:1, :], inside)
    a1[N1:, :] = jnp.zeros((8, LANES), F32)
    pad_back[...] = jnp.zeros_like(pad_back)
    for t in range(9):
        store_weight(w2, t, w_second[t].T)
        store_weight(w1_back, t, padded_rows(pad_back, w_first[8 - t]).T)


def forward_kernel(core, half, consts, centre, a1_part, slopes_part, outer, inner, w1, w2, cells, a1, s1, s2, small, send, edge, high, low, high1, low1, high2, low2):
    west = half[0] == 0
    b1, b2 = consts[0:1, :], consts[1:2, :]
    weights = [consts[6:7, i : i + 1] for i in range(ROWS + 6)]
    a1[...] = a1_part[...]
    for i in range(ROWS + 2):
        r = (i + 2) * PITCH + 6
        s1[i * SHORT : (i + 1) * SHORT, :] = slopes_part[r : r + SHORT, :]
    cells[...] = centre[3 * PITCH : 21 * PITCH + 8, :]
    edge[...] = jnp.zeros_like(edge)
    for i in range(ROWS + 8):
        r, q = i * PITCH, i * NARROW
        before = jnp.where(west, outer[i], inner[i])
        after = jnp.where(west, inner[i], outer[i])
        edge[q : q + 4, :CIN] = before
        edge[q + 4 : q + 6, :] = centre[r + 8 : r + 10, :]
        edge[q + 8 : q + 10, :] = centre[r + 6 + COLS : r + 8 + COLS, :]
        edge[q + 10 : q + 14, :CIN] = after
        if 3 <= i < 21:
            r = (i - 3) * PITCH
            cells[r + 4 : r + 8, :CIN] = before
            cells[r + 8 + COLS : r + 12 + COLS, :CIN] = after
    spread_packed(edge, high1, low1, ROWS + 8, width=NARROW, pitch=NARROW)
    acc = convolve(high1, low1, w1, 0, ROWS + 6, NARROW)
    for i in range(ROWS + 6):
        r = i * PITCH
        inside = jnp.where(weights[i] > 0.0, 1.0, 0.0)
        active, slope = activate(acc[i * NARROW : (i + 1) * NARROW] + b1, inside)
        a1[r + 4 : r + 8, :] = active[:4]
        a1[r + 6 + COLS : r + 10 + COLS, :] = active[8:12]
        if 2 <= i < ROWS + 4:
            r = (i - 2) * SHORT
            s1[r : r + 2, :] = slope[2:4]
            s1[r + COLS : r + COLS + 3, :] = slope[8:11]
    spread(a1, high, low, ROWS + 6)
    mask = column_mask(6, (PITCH, LANES))
    pooled = jnp.zeros((PITCH, LANES), F32)
    bias = jnp.zeros((PITCH, LANES), F32)
    for first, rows in chunks(ROWS + 4, 2):
        acc = convolve(high, low, w2, first, rows)
        for k in range(rows):
            i = first + k
            r = i * PITCH
            h = acc[k * PITCH : (k + 1) * PITCH] + b2
            sigma = jax.nn.sigmoid(h)
            weight = weights[i + 1]
            slope = sigma * (1.0 + h * (1.0 - sigma)) * weight
            s2[r : r + PITCH, :] = slope
            if 2 <= i < ROWS + 2:
                pooled = pooled + h * sigma * weight
                bias = bias + slope
    s2[N2:, :] = jnp.zeros((8, LANES), F32)
    small[0:1, :] = jnp.sum(pooled * mask, axis=0, keepdims=True)
    small[1:2, :] = jnp.sum(bias * mask, axis=0, keepdims=True)
    correlate_half(1 - core[0], a1, s2, high2, low2, send)
    send[HALF : HALF + 2, :] = small[...]


def write_pieces(out, rows):
    count, size = out.shape[0], out.shape[1]
    for p in range(count):
        q = (p % 2) * (count // 2) + p // 2
        out[p] = rows[q * size : (q + 1) * size, :]


def second_kernel(core, a1, s2, out, high, low):
    correlate_half(core[0], a1, s2, high, low, out)


def pair_kernel(own, other, small, out):
    size = out.shape[1] - 2
    sums = small[...] + other[HALF : HALF + 2, :]
    for p in range(out.shape[0]):
        r = slice(p * size, (p + 1) * size)
        out[p, :size] = own[r, :] + other[r, :]
        out[p, size:] = sums


def mode_gradients(sums, modes, consts):
    total = jnp.sum(sums[...], axis=0)
    pooled = total[0:1]
    amplitude = jnp.sum(modes[...] * pooled, axis=1, keepdims=True)
    count = amplitude.shape[0]
    cotangent = jnp.concatenate(
        [jnp.broadcast_to(consts[k : k + 1, :], (LANES, LANES)).T[:, :1] for k in range(2, 2 + count // LANES)], axis=0
    )
    width = jnp.sqrt(jnp.sum(amplitude * amplitude, axis=0, keepdims=True) / count + 1e-05)
    normal = amplitude / width
    along = jnp.sum(cotangent * normal, axis=0, keepdims=True) / count
    d_amplitude = (cotangent - normal * along) / width
    d_pooled = jnp.sum(d_amplitude * modes[...], axis=0, keepdims=True)
    return total, pooled, d_amplitude, d_pooled


def share_kernel(parts, out):
    total = jnp.sum(parts[...], axis=0)
    bit, size = out.shape[1] - 2, total.shape[0] - 2
    for z in range(out.shape[0]):
        out[z] = jnp.zeros_like(out[z])
        out[z, :2] = total[size:]
        count = min(bit, size - z * bit)
        if count > 0:
            out[z, 2 : 2 + count] = total[z * bit : z * bit + count]


def ring_kernel(parts, sums, out):
    part = jnp.sum(parts[...], axis=0)
    bit = jnp.sum(sums[...], axis=0)[2:]
    for z in range(out.shape[0]):
        out[z, : part.shape[0]] = part
        out[z, part.shape[0] :] = bit


def plane_kernel(size, both, out, rows):
    first = out.shape[1] - size
    part = jnp.sum(both[...], axis=0)[:first]
    bit = both.shape[1] - first
    for z in range(-(-size // bit)):
        count = min(bit, size - z * bit)
        rows[z * bit : z * bit + count, :] = both[z, first : first + count]
    second = rows[...]
    for p in range(out.shape[0]):
        out[p, :size] = second
        out[p, size:] = part


def backward_kernel(sums, modes, consts, s1, s2, x, w_second, out, g1, weight, rows, high, low, high1, low1):
    spread(s2, high, low, ROWS + 4, col=4, width=SHORT)
    d_pooled = mode_gradients(sums, modes, consts)[3]
    column = jnp.broadcast_to(d_pooled, (LANES, LANES)).T
    for t in range(9):
        store_weight(weight, t, w_second[8 - t] * column)
    for first, count in chunks(ROWS + 2, 3):
        r = slice(first * SHORT, (first + count) * SHORT)
        g1[r, :] = convolve(high, low, weight, first, count, SHORT) * s1[r, :]
    g1[N3:, :] = jnp.zeros((8, LANES), F32)

    mask = column_mask(1, (SHORT, LANES))
    own = [g1[(i + 1) * SHORT : (i + 2) * SHORT, :] * mask for i in range(ROWS)]
    bias1 = own[0]
    for row in own[1:]:
        bias1 = bias1 + row
    grad = jnp.concatenate(own + [jnp.zeros((SHORT, LANES), F32)], axis=0)
    spread_packed(x, high1, low1, 18, col=6, width=SHORT)
    for a, block in enumerate(correlate(grad, high1, low1, [(a, 0, 2 * LANES) for a in range(3)])):
        rows[3 * a * CIN : 3 * (a + 1) * CIN, :] = block.T[: 3 * CIN]
    rows[9 * CIN : 9 * CIN + 1, :] = jnp.sum(bias1, axis=0, keepdims=True)
    rows[9 * CIN + 1 :, :] = jnp.zeros((rows.shape[0] - 9 * CIN - 1, LANES), F32)
    write_pieces(out, rows)


def field_kernel(scale, g1, weight, sums, modes, consts, out, d_modes, spread_d, bias2, high, low):
    total, pooled, d_amplitude, d_pooled = mode_gradients(sums, modes, consts)
    d_modes[...] = d_amplitude * pooled
    spread_d[...] = jnp.broadcast_to(d_pooled, (LANES, LANES)).T
    bias2[...] = total[1:2] * d_pooled
    spread(g1, high, low, ROWS + 2, width=SHORT, pitch=SHORT)
    for first, count in chunks(ROWS, 2):
        acc = convolve(high, low, weight, first, count, SHORT) * scale
        for k in range(count):
            out[first + k] = acc[k * SHORT : k * SHORT + COLS, :CIN]


def finish_kernel(core, mine, other, spread_d, w_second, w_first, b_first, rows):
    chips = mine.shape[0]
    size = HALF // chips
    rest = mine.shape[1] - size
    even = core[0] == 0

    def gather(start, count):
        for p in range(chips):
            m, o = mine[p, start : start + count, :], other[p, start : start + count, :]
            rows[p * count : (p + 1) * count, :] = jnp.where(even, m, o)
            rows[(chips + p) * count : (chips + p + 1) * count, :] = jnp.where(even, o, m)

    gather(0, size)
    for t in range(9):
        w_second[t] = rows[t * LANES : (t + 1) * LANES, :] * spread_d[...]
    gather(size, rest)
    for t in range(9):
        w_first[t] = rows[t * CIN : (t + 1) * CIN, :]
    b_first[...] = rows[9 * CIN : 9 * CIN + 1, :]


def call(kernel, outs, scratch, flops, smem=()):
    outs = [o if isinstance(o[0], tuple) else (o, F32) for o in outs]

    def run(*args):
        return pl.pallas_call(
            kernel,
            out_shape=[jax.ShapeDtypeStruct(s, d) for s, d in outs],
            in_specs=[pl.BlockSpec(memory_space=pltpu.SMEM if i in smem else pltpu.VMEM) for i in range(len(args))],
            out_specs=[pl.BlockSpec(memory_space=pltpu.VMEM) for _ in outs],
            scratch_shapes=[pltpu.VMEM(s, d) for s, d in scratch],
            compiler_params=pltpu.CompilerParams(vmem_limit_bytes=12 << 20),
            cost_estimate=pl.CostEstimate(flops=flops, bytes_accessed=4 << 20, transcendentals=0),
        )(*args)

    return run


def far_pairs(count, closed):
    pairs = [(i, (i + 1) % count) for i in range(1, count if closed else count - 1, 2)]
    return pairs + [(j, i) for i, j in pairs]


def near_pairs(count):
    pairs = [(i, i + 1) for i in range(0, count, 2)]
    return pairs + [(j, i) for i, j in pairs]


def row_weights(first, count, nlat, nlon):
    phi = (np.arange(nlat) + 0.5) * (math.pi / nlat) - math.pi / 2
    total = float(np.cos(phi).sum() * nlon)
    row = first + jnp.arange(count, dtype=jnp.int32)
    phi = (row.astype(F32) + 0.5) * (math.pi / nlat) - math.pi / 2
    return jnp.where((row >= 0) & (row < nlat), jnp.cos(phi), 0.0) / total


def swap(pieces, axes):
    return lax.all_to_all(pieces, axes, 0, 0, tiled=True)


def body(field, w_first, b_first, w_second, b_second, modes, cotangent):
    cin, rows, cols = field.shape
    ch = w_first.shape[1]
    n_lat, n_lon = lax.axis_size(LAT), lax.axis_size(LON)
    n_pl, n_z = lax.axis_size(PLANE), lax.axis_size(RING)
    nlat, nlon = rows * n_lat, cols * n_lon
    weights = row_weights(lax.axis_index(LAT) * rows - 3, LANES, nlat, nlon)
    consts = jnp.concatenate([b_first, b_second, cotangent, weights]).reshape(-1, LANES)

    own = field.transpose(1, 2, 0)
    core, half = lax.axis_index("c"), lax.axis_index("xh")
    inner = lax.ppermute(lax.dynamic_slice_in_dim(own, (1 - core) * (rows - 4), 4, 0), LAT, near_pairs(n_lat))
    outer = lax.ppermute(lax.dynamic_slice_in_dim(own, core * (rows - 4), 4, 0), LAT, far_pairs(n_lat, False))
    strips = []
    for start in (half * (cols - 4), (1 - half) * (cols - 4)):
        a, b, c = [lax.dynamic_slice_in_dim(v, start, 4, 1) for v in (outer, own, inner)]
        strips.append(jnp.concatenate([jnp.where(core == 0, a, c), b, jnp.where(core == 0, c, a)], axis=0))
    outer_strip = lax.ppermute(strips[0], LON, far_pairs(n_lon, True))
    inner_strip = lax.ppermute(strips[1], LON, near_pairs(n_lon))
    core, half = core.astype(jnp.int32).reshape(1), half.astype(jnp.int32).reshape(1)
    w_first = w_first.transpose(0, 2, 1)
    weight = ((3, 3 * LANES, 2 * LANES), BF16)
    packed = ((3, 2 * LANES, 2 * LANES), BF16)
    pad = ((LANES, LANES), F32)
    pair = lambda n, width=3 * LANES: [((n, width), BF16), ((n, width), BF16)]
    centre, a1, slopes, w1, w2, w1_back = call(
        prepare_kernel,
        [(NX + 8, LANES), (N1 + 8, LANES), (N1, LANES), packed, weight, weight],
        [((2 * LANES, LANES), F32), pad] + pair(NX, 2 * LANES),
        10**9,
        smem=(0,),
    )(core, consts, own, inner, outer, w_first, w_second)
    swap_cores = lambda v: lax.ppermute(v, "c", [(0, 1), (1, 0)])
    x, a1, s1, s2, small, send = call(
        forward_kernel,
        [(18 * PITCH + 8, LANES), (N1 + 8, LANES), (N3, LANES), (N2 + 8, LANES), (2, LANES), (HALF + 8, LANES)],
        [((23 * NARROW + 8, LANES), F32)]
        + pair(N1)
        + pair(23 * NARROW, 2 * LANES)
        + pair(18 * SHORT),
        10**9,
        smem=(0, 1),
    )(core, half, consts, centre, a1, slopes, outer_strip, inner_strip, w1, w2)

    other = swap_cores(send)
    (half,) = call(second_kernel, [(HALF, LANES)], pair(18 * SHORT), 10**9, smem=(0,))(core, a1, s2)
    share2 = HALF * 2 // n_pl
    (part,) = call(pair_kernel, [(n_pl // 2, share2 + 2, ch)], [], 10**6)(half, other, small)
    bit2 = -(-share2 // n_z)
    (mine,) = call(share_kernel, [(n_z, bit2 + 2, ch)], [], 10**6)(swap(part, CHIPS))
    mine = swap(mine, RING)

    share1 = -(-(9 * cin + 1) // n_pl)
    g1rows, g1 = call(
        backward_kernel,
        [(n_pl, share1, ch), (N3 + 8, LANES)],
        [weight, ((n_pl * share1, LANES), F32)] + pair(19 * SHORT) + pair(18 * SHORT, 2 * LANES),
        10**9,
    )(mine, modes, consts, s1, s2, x, w_second)

    part = swap(g1rows, PLANE)
    (both,) = call(ring_kernel, [(n_z, share1 + bit2, ch)], [], 10**6)(part, mine)
    (whole,) = call(
        lambda *r: plane_kernel(share2, *r), [(n_pl // 2, share2 + share1, ch)], [((share2, LANES), F32)], 10**6
    )(swap(both, RING))
    whole = swap(whole, CHIPS)
    whole, g1 = lax.optimization_barrier((whole, g1))
    other = swap_cores(whole)
    grad_field, d_modes, spread_d, bias2 = call(
        lambda *r: field_kernel(float(nlat * nlon), *r),
        [(rows, cols, cin), modes.shape, (LANES, LANES), (1, LANES)],
        pair(N3),
        10**9,
    )(g1, w1_back, mine, modes, consts)
    grad_w_second, grad_w_first, grad_b_first = call(
        finish_kernel,
        [(9, ch, ch), (9, cin, ch), (1, ch)],
        [((2 * HALF, LANES), F32)],
        10**6,
        smem=(0,),
    )(core, whole, other, spread_d)
    return (grad_field.transpose(2, 0, 1), grad_w_first.transpose(0, 2, 1), grad_b_first[0], grad_w_second, bias2[0], d_modes)


def solution(mesh):
    fine = Mesh(mesh.devices.reshape(4, 2, 2, 16, 2), ("y", "xl", "c", "z", "xh"))
    in_specs = (P(None, LAT, LON), P(), P(), P(), P(), P(), P())
    out_specs = (P(None, LAT, LON), P(), P(), P(), P(), P())
    return jax.shard_map(body, mesh=fine, in_specs=in_specs, out_specs=out_specs, check_vma=False)
```

```python
import math

import jax
import jax.numpy as jnp
import numpy as np
from jax import lax
from jax.experimental import pallas as pl
from jax.experimental.pallas import tpu as pltpu
from jax.sharding import Mesh, PartitionSpec as P

LAT = ("y", "xl", "c")
LON = ("z", "xh")
CHIPS = ("y", "xl", "xh")
PLANE = ("y", "xl", "xh", "c")
RING = ("z",)
F32 = jnp.float32
BF16 = jnp.bfloat16

PITCH = 64
LANES = 128
ROWS, COLS, CIN = 15, 45, 69
SHORT = 48
NARROW = 16
PAIRS = 46
WINDOW = 16 * SHORT
NX, N1, N2, N3 = 23 * PITCH, 21 * PITCH, 19 * PITCH, 17 * SHORT


def split(x):
    hi = x.astype(BF16)
    return hi, (x - hi.astype(F32)).astype(BF16)


def spread(src, high, low, rows, first=0, col=0, width=PITCH, pitch=PITCH):
    for i in range(rows):
        for b in range(3):
            r = (first + i) * pitch + col + b
            hi, lo = split(src[r : r + width, :])
            high[i * width : (i + 1) * width, b * LANES : (b + 1) * LANES] = hi
            low[i * width : (i + 1) * width, b * LANES : (b + 1) * LANES] = lo


def spread_packed(src, high, low, rows, col=0, width=PITCH, pitch=PITCH):
    lane = lax.broadcasted_iota(jnp.int32, (width, LANES), 1)
    for i in range(rows):
        r = i * pitch + col
        second = pltpu.roll(src[r + 1 : r + 1 + width, :], CIN, 1)
        third = pltpu.roll(src[r + 2 : r + 2 + width, :], 2 * CIN - LANES, 1)
        for k, x in enumerate(
            (jnp.where(lane < CIN, src[r : r + width, :], second), jnp.where(lane < 2 * CIN - LANES, second, third))
        ):
            hi, lo = split(x)
            high[i * width : (i + 1) * width, k * LANES : (k + 1) * LANES] = hi
            low[i * width : (i + 1) * width, k * LANES : (k + 1) * LANES] = lo


def dot(a, b):
    return jnp.dot(a, b, preferred_element_type=F32)


def convolve(high, low, weight, first, rows, pitch=PITCH):
    def taps(src):
        return jnp.concatenate([src[(first + a) * pitch : (first + a + rows) * pitch, :] for a in range(3)], axis=1)

    w = jnp.concatenate([weight[a] for a in range(3)], axis=0)
    both = dot(taps(high), w)
    return both[:, :LANES] + both[:, LANES:] + dot(taps(low), w[:, :LANES])


def correlate(grad, high, low, spans):
    hi, lo = split(grad.T)
    both = jnp.concatenate([hi, lo], axis=0)
    blocks = []
    for a, first, last in spans:
        r = slice(a * SHORT, a * SHORT + WINDOW)
        out = dot(both, high[r, first:last])
        blocks.append(out[:LANES] + out[LANES:] + dot(hi, low[r, first:last]))
    return blocks


HALVES = (((0, 0, 3 * LANES), (1, 0, 2 * LANES)), ((1, LANES, 3 * LANES), (2, 0, 3 * LANES)))
HALF = 9 * LANES // 2


def correlate_half(core, a1, s2, high, low, out):
    spread(a1, high, low, 18, first=2, col=6, width=SHORT)
    mask = column_mask(0, (SHORT, LANES))
    own = [s2[(i + 2) * PITCH + 6 : (i + 2) * PITCH + 6 + SHORT, :] * mask for i in range(ROWS)]
    grad = jnp.concatenate(own + [jnp.zeros((SHORT, LANES), F32)], axis=0)
    for half in range(2):

        @pl.when(core == half)
        def _():
            r = -half * (LANES // 2)
            for block in correlate(grad, high, low, HALVES[half]):
                for k in range(0, block.shape[1], LANES):
                    first, last = max(r, 0), min(r + LANES, HALF)
                    out[first:last, :] = block[first - r : last - r, k : k + LANES]
                    r += LANES


def chunks(rows, parts):
    size = -(-rows // parts)
    return [(s, min(size, rows - s)) for s in range(0, rows, size)]


def column_mask(first, shape):
    col = lax.broadcasted_iota(jnp.int32, shape, 0)
    return ((col >= first) & (col < first + COLS)).astype(F32)


def padded_rows(pad, block):
    pad[:CIN, :] = block
    return pad[...]


def store_weight(weight, t, block):
    a, b = t // 3, t % 3
    hi, lo = split(block)
    weight[a, b * LANES : (b + 1) * LANES, :LANES] = hi
    weight[a, b * LANES : (b + 1) * LANES, LANES:] = lo


def pack_kernel(core, half, own, outer, inner, far, near, strip):
    upper, west = core[0] == 0, half[0] == 0
    lane = lax.broadcasted_iota(jnp.int32, (PAIRS, LANES), 1)
    strip[...] = jnp.zeros_like(strip)
    for out, first in ((far, True), (near, False)):
        for i in range(ROWS + 8):
            left, right = slice(0, 4), slice(COLS - 4, COLS)
            if not first:
                left, right = right, left
            if 4 <= i < ROWS + 4:
                cells = jnp.where(west, own[i - 4, left], own[i - 4, right])
            else:
                k = i if i < 4 else i - ROWS - 4
                a, b = (outer, inner) if i < 4 else (inner, outer)
                cells = jnp.where(upper, jnp.where(west, a[k, left], a[k, right]), jnp.where(west, b[k, left], b[k, right]))
            strip[4 * i : 4 * i + 4, :CIN] = cells
        moved = pltpu.roll(strip[...], LANES // 2, 1)
        out[:PAIRS, :] = jnp.where(lane < LANES // 2, strip[:PAIRS, :], moved[PAIRS : 2 * PAIRS])
        out[PAIRS : PAIRS + 2, :] = jnp.zeros((2, LANES), F32)
        out[PAIRS + 2 :, :] = moved.T[:8]


def unpack(packed, block):
    block[:8, :] = packed[PAIRS + 2 :, :]
    last = pltpu.roll(block[...].T, LANES // 2, 1)[: 2 * PAIRS]
    most = jnp.concatenate([packed[:PAIRS, :], pltpu.roll(packed[:PAIRS, :], LANES // 2, 1)], axis=0)
    lane = lax.broadcasted_iota(jnp.int32, (2 * PAIRS, LANES), 1)
    return jnp.where(lane < LANES // 2, most, last)


def activate(h, inside):
    sigma = jax.nn.sigmoid(h)
    return h * sigma * inside, sigma * (1.0 + h * (1.0 - sigma)) * inside


def prepare_kernel(core, consts, own, inner, outer, w_first, w_second, x, a1, slopes, w1, w2, w1_back, pad, pad_back, high, low):
    upper = core[0] == 0
    x[...] = jnp.zeros_like(x)
    for i in range(ROWS + 8):
        r = i * PITCH
        if i < 4:
            row = jnp.where(upper, outer[i], inner[i])
        elif i < ROWS + 4:
            row = own[i - 4]
        else:
            row = jnp.where(upper, inner[i - ROWS - 4], outer[i - ROWS - 4])
        x[r + 8 : r + 8 + COLS, :CIN] = row
    pad[...] = jnp.zeros_like(pad)
    for a in range(3):
        for b in range(3):
            pad[b * CIN : (b + 1) * CIN, :] = w_first[3 * a + b]
        hi, lo = split(pad[...])
        w1[a, :, :LANES] = hi
        w1[a, :, LANES:] = lo
    spread_packed(x, high, low, ROWS + 8)
    for first, rows in chunks(ROWS + 6, 2):
        acc = convolve(high, low, w1, first, rows)
        for k in range(rows):
            i = first + k
            inside = jnp.where(consts[6:7, i : i + 1] > 0.0, 1.0, 0.0)
            r = slice(i * PITCH, (i + 1) * PITCH)
            a1[r, :], slopes[r, :] = activate(acc[k * PITCH : (k + 1) * PITCH] + consts[0:1, :], inside)
    a1[N1:, :] = jnp.zeros((8, LANES), F32)
    pad_back[...] = jnp.zeros_like(pad_back)
    for t in range(9):
        store_weight(w2, t, w_second[t].T)
        store_weight(w1_back, t, padded_rows(pad_back, w_first[8 - t]).T)


def forward_kernel(core, half, consts, centre, a1_part, slopes_part, outer, inner, w1, w2, cells, a1, s1, s2, small, send, edge, block, strip, high, low, high1, low1, high2, low2):
    west = half[0] == 0
    b1, b2 = consts[0:1, :], consts[1:2, :]
    weights = [consts[6:7, i : i + 1] for i in range(ROWS + 6)]
    a1[...] = a1_part[...]
    for i in range(ROWS + 2):
        r = (i + 2) * PITCH + 6
        s1[i * SHORT : (i + 1) * SHORT, :] = slopes_part[r : r + SHORT, :]
    cells[...] = centre[3 * PITCH : 21 * PITCH + 8, :]
    edge[...] = jnp.zeros_like(edge)
    block[...] = jnp.zeros_like(block)
    far = unpack(outer, block)
    near = unpack(inner, block)
    strip[0] = jnp.where(west, far, near)
    strip[1] = jnp.where(west, near, far)
    for i in range(ROWS + 8):
        r, q = i * PITCH, i * NARROW
        before, after = strip[0, 4 * i : 4 * i + 4], strip[1, 4 * i : 4 * i + 4]
        edge[q : q + 4, :] = before
        edge[q + 4 : q + 6, :] = centre[r + 8 : r + 10, :]
        edge[q + 8 : q + 10, :] = centre[r + 6 + COLS : r + 8 + COLS, :]
        edge[q + 10 : q + 14, :] = after
        if 3 <= i < 21:
            r = (i - 3) * PITCH
            cells[r + 4 : r + 8, :] = before
            cells[r + 8 + COLS : r + 12 + COLS, :] = after
    spread_packed(edge, high1, low1, ROWS + 8, width=NARROW, pitch=NARROW)
    acc = convolve(high1, low1, w1, 0, ROWS + 6, NARROW)
    for i in range(ROWS + 6):
        r = i * PITCH
        inside = jnp.where(weights[i] > 0.0, 1.0, 0.0)
        active, slope = activate(acc[i * NARROW : (i + 1) * NARROW] + b1, inside)
        a1[r + 4 : r + 8, :] = active[:4]
        a1[r + 6 + COLS : r + 10 + COLS, :] = active[8:12]
        if 2 <= i < ROWS + 4:
            r = (i - 2) * SHORT
            s1[r : r + 2, :] = slope[2:4]
            s1[r + COLS : r + COLS + 3, :] = slope[8:11]
    spread(a1, high, low, ROWS + 6)
    mask = column_mask(6, (PITCH, LANES))
    pooled = jnp.zeros((PITCH, LANES), F32)
    bias = jnp.zeros((PITCH, LANES), F32)
    for first, rows in chunks(ROWS + 4, 2):
        acc = convolve(high, low, w2, first, rows)
        for k in range(rows):
            i = first + k
            r = i * PITCH
            h = acc[k * PITCH : (k + 1) * PITCH] + b2
            sigma = jax.nn.sigmoid(h)
            weight = weights[i + 1]
            slope = sigma * (1.0 + h * (1.0 - sigma)) * weight
            s2[r : r + PITCH, :] = slope
            if 2 <= i < ROWS + 2:
                pooled = pooled + h * sigma * weight
                bias = bias + slope
    s2[N2:, :] = jnp.zeros((8, LANES), F32)
    small[0:1, :] = jnp.sum(pooled * mask, axis=0, keepdims=True)
    small[1:2, :] = jnp.sum(bias * mask, axis=0, keepdims=True)
    correlate_half(1 - core[0], a1, s2, high2, low2, send)
    send[HALF : HALF + 2, :] = small[...]


def write_pieces(out, rows):
    count, size = out.shape[0], out.shape[1]
    for p in range(count):
        q = (p % 2) * (count // 2) + p // 2
        out[p] = rows[q * size : (q + 1) * size, :]


def second_kernel(core, a1, s2, out, high, low):
    correlate_half(core[0], a1, s2, high, low, out)


def pair_kernel(own, other, small, out):
    size = out.shape[1] - 2
    sums = small[...] + other[HALF : HALF + 2, :]
    for p in range(out.shape[0]):
        r = slice(p * size, (p + 1) * size)
        out[p, :size] = own[r, :] + other[r, :]
        out[p, size:] = sums


def mode_gradients(sums, modes, consts):
    total = jnp.sum(sums[...], axis=0)
    pooled = total[0:1]
    amplitude = jnp.sum(modes[...] * pooled, axis=1, keepdims=True)
    count = amplitude.shape[0]
    cotangent = jnp.concatenate(
        [jnp.broadcast_to(consts[k : k + 1, :], (LANES, LANES)).T[:, :1] for k in range(2, 2 + count // LANES)], axis=0
    )
    width = jnp.sqrt(jnp.sum(amplitude * amplitude, axis=0, keepdims=True) / count + 1e-05)
    normal = amplitude / width
    along = jnp.sum(cotangent * normal, axis=0, keepdims=True) / count
    d_amplitude = (cotangent - normal * along) / width
    d_pooled = jnp.sum(d_amplitude * modes[...], axis=0, keepdims=True)
    return total, pooled, d_amplitude, d_pooled


def share_kernel(parts, out):
    total = jnp.sum(parts[...], axis=0)
    bit, size = out.shape[1] - 2, total.shape[0] - 2
    for z in range(out.shape[0]):
        out[z] = jnp.zeros_like(out[z])
        out[z, :2] = total[size:]
        count = min(bit, size - z * bit)
        if count > 0:
            out[z, 2 : 2 + count] = total[z * bit : z * bit + count]


def ring_kernel(parts, sums, out):
    part = jnp.sum(parts[...], axis=0)
    bit = jnp.sum(sums[...], axis=0)[2:]
    for z in range(out.shape[0]):
        out[z, : part.shape[0]] = part
        out[z, part.shape[0] :] = bit


def plane_kernel(size, both, out, rows):
    first = out.shape[1] - size
    part = jnp.sum(both[...], axis=0)[:first]
    bit = both.shape[1] - first
    for z in range(-(-size // bit)):
        count = min(bit, size - z * bit)
        rows[z * bit : z * bit + count, :] = both[z, first : first + count]
    second = rows[...]
    for p in range(out.shape[0]):
        out[p, :size] = second
        out[p, size:] = part


def backward_kernel(sums, modes, consts, s1, s2, x, w_second, out, g1, weight, rows, high, low, high1, low1):
    spread(s2, high, low, ROWS + 4, col=4, width=SHORT)
    d_pooled = mode_gradients(sums, modes, consts)[3]
    column = jnp.broadcast_to(d_pooled, (LANES, LANES)).T
    for t in range(9):
        store_weight(weight, t, w_second[8 - t] * column)
    for first, count in chunks(ROWS + 2, 3):
        r = slice(first * SHORT, (first + count) * SHORT)
        g1[r, :] = convolve(high, low, weight, first, count, SHORT) * s1[r, :]
    g1[N3:, :] = jnp.zeros((8, LANES), F32)

    mask = column_mask(1, (SHORT, LANES))
    own = [g1[(i + 1) * SHORT : (i + 2) * SHORT, :] * mask for i in range(ROWS)]
    bias1 = own[0]
    for row in own[1:]:
        bias1 = bias1 + row
    grad = jnp.concatenate(own + [jnp.zeros((SHORT, LANES), F32)], axis=0)
    spread_packed(x, high1, low1, 18, col=6, width=SHORT)
    for a, block in enumerate(correlate(grad, high1, low1, [(a, 0, 2 * LANES) for a in range(3)])):
        rows[3 * a * CIN : 3 * (a + 1) * CIN, :] = block.T[: 3 * CIN]
    rows[9 * CIN : 9 * CIN + 1, :] = jnp.sum(bias1, axis=0, keepdims=True)
    rows[9 * CIN + 1 :, :] = jnp.zeros((rows.shape[0] - 9 * CIN - 1, LANES), F32)
    write_pieces(out, rows)


def field_kernel(scale, g1, weight, sums, modes, consts, out, d_modes, spread_d, bias2, high, low):
    total, pooled, d_amplitude, d_pooled = mode_gradients(sums, modes, consts)
    d_modes[...] = d_amplitude * pooled
    spread_d[...] = jnp.broadcast_to(d_pooled, (LANES, LANES)).T
    bias2[...] = total[1:2] * d_pooled
    spread(g1, high, low, ROWS + 2, width=SHORT, pitch=SHORT)
    for first, count in chunks(ROWS, 2):
        acc = convolve(high, low, weight, first, count, SHORT) * scale
        for k in range(count):
            out[first + k] = acc[k * SHORT : k * SHORT + COLS, :CIN]


def finish_kernel(core, mine, other, spread_d, w_second, w_first, b_first, rows):
    chips = mine.shape[0]
    size = HALF // chips
    rest = mine.shape[1] - size
    even = core[0] == 0

    def gather(start, count):
        for p in range(chips):
            m, o = mine[p, start : start + count, :], other[p, start : start + count, :]
            rows[p * count : (p + 1) * count, :] = jnp.where(even, m, o)
            rows[(chips + p) * count : (chips + p + 1) * count, :] = jnp.where(even, o, m)

    gather(0, size)
    for t in range(9):
        w_second[t] = rows[t * LANES : (t + 1) * LANES, :] * spread_d[...]
    gather(size, rest)
    for t in range(9):
        w_first[t] = rows[t * CIN : (t + 1) * CIN, :]
    b_first[...] = rows[9 * CIN : 9 * CIN + 1, :]


def call(kernel, outs, scratch, flops, smem=()):
    outs = [o if isinstance(o[0], tuple) else (o, F32) for o in outs]

    def run(*args):
        return pl.pallas_call(
            kernel,
            out_shape=[jax.ShapeDtypeStruct(s, d) for s, d in outs],
            in_specs=[pl.BlockSpec(memory_space=pltpu.SMEM if i in smem else pltpu.VMEM) for i in range(len(args))],
            out_specs=[pl.BlockSpec(memory_space=pltpu.VMEM) for _ in outs],
            scratch_shapes=[pltpu.VMEM(s, d) for s, d in scratch],
            compiler_params=pltpu.CompilerParams(vmem_limit_bytes=12 << 20),
            cost_estimate=pl.CostEstimate(flops=flops, bytes_accessed=4 << 20, transcendentals=0),
        )(*args)

    return run


def far_pairs(count, closed):
    pairs = [(i, (i + 1) % count) for i in range(1, count if closed else count - 1, 2)]
    return pairs + [(j, i) for i, j in pairs]


def near_pairs(count):
    pairs = [(i, i + 1) for i in range(0, count, 2)]
    return pairs + [(j, i) for i, j in pairs]


def row_weights(first, count, nlat, nlon):
    phi = (np.arange(nlat) + 0.5) * (math.pi / nlat) - math.pi / 2
    total = float(np.cos(phi).sum() * nlon)
    row = first + jnp.arange(count, dtype=jnp.int32)
    phi = (row.astype(F32) + 0.5) * (math.pi / nlat) - math.pi / 2
    return jnp.where((row >= 0) & (row < nlat), jnp.cos(phi), 0.0) / total


def swap(pieces, axes):
    return lax.all_to_all(pieces, axes, 0, 0, tiled=True)


def body(field, w_first, b_first, w_second, b_second, modes, cotangent):
    cin, rows, cols = field.shape
    ch = w_first.shape[1]
    n_lat, n_lon = lax.axis_size(LAT), lax.axis_size(LON)
    n_pl, n_z = lax.axis_size(PLANE), lax.axis_size(RING)
    nlat, nlon = rows * n_lat, cols * n_lon
    weights = row_weights(lax.axis_index(LAT) * rows - 3, LANES, nlat, nlon)
    consts = jnp.concatenate([b_first, b_second, cotangent, weights]).reshape(-1, LANES)

    own = field.transpose(1, 2, 0)
    core, half = lax.axis_index("c"), lax.axis_index("xh")
    inner = lax.ppermute(lax.dynamic_slice_in_dim(own, (1 - core) * (rows - 4), 4, 0), LAT, near_pairs(n_lat))
    outer = lax.ppermute(lax.dynamic_slice_in_dim(own, core * (rows - 4), 4, 0), LAT, far_pairs(n_lat, False))
    core, half = core.astype(jnp.int32).reshape(1), half.astype(jnp.int32).reshape(1)
    strips = call(pack_kernel, [(PAIRS + 10, LANES)] * 2, [((LANES, LANES), F32)], 10**6, smem=(0, 1))(
        core, half, own, outer, inner
    )
    outer_strip = lax.ppermute(strips[0], LON, far_pairs(n_lon, True))
    inner_strip = lax.ppermute(strips[1], LON, near_pairs(n_lon))
    w_first = w_first.transpose(0, 2, 1)
    weight = ((3, 3 * LANES, 2 * LANES), BF16)
    packed = ((3, 2 * LANES, 2 * LANES), BF16)
    pad = ((LANES, LANES), F32)
    pair = lambda n, width=3 * LANES: [((n, width), BF16), ((n, width), BF16)]
    centre, a1, slopes, w1, w2, w1_back = call(
        prepare_kernel,
        [(NX + 8, LANES), (N1 + 8, LANES), (N1, LANES), packed, weight, weight],
        [((2 * LANES, LANES), F32), pad] + pair(NX, 2 * LANES),
        10**9,
        smem=(0,),
    )(core, consts, own, inner, outer, w_first, w_second)
    swap_cores = lambda v: lax.ppermute(v, "c", [(0, 1), (1, 0)])
    x, a1, s1, s2, small, send = call(
        forward_kernel,
        [(18 * PITCH + 8, LANES), (N1 + 8, LANES), (N3, LANES), (N2 + 8, LANES), (2, LANES), (HALF + 8, LANES)],
        [((23 * NARROW + 8, LANES), F32), ((LANES, LANES), F32), ((2, 2 * PAIRS, LANES), F32)]
        + pair(N1)
        + pair(23 * NARROW, 2 * LANES)
        + pair(18 * SHORT),
        10**9,
        smem=(0, 1),
    )(core, half, consts, centre, a1, slopes, outer_strip, inner_strip, w1, w2)

    other = swap_cores(send)
    (half,) = call(second_kernel, [(HALF, LANES)], pair(18 * SHORT), 10**9, smem=(0,))(core, a1, s2)
    share2 = HALF * 2 // n_pl
    (part,) = call(pair_kernel, [(n_pl // 2, share2 + 2, ch)], [], 10**6)(half, other, small)
    bit2 = -(-share2 // n_z)
    (mine,) = call(share_kernel, [(n_z, bit2 + 2, ch)], [], 10**6)(swap(part, CHIPS))
    mine = swap(mine, RING)

    share1 = -(-(9 * cin + 1) // n_pl)
    g1rows, g1 = call(
        backward_kernel,
        [(n_pl, share1, ch), (N3 + 8, LANES)],
        [weight, ((n_pl * share1, LANES), F32)] + pair(19 * SHORT) + pair(18 * SHORT, 2 * LANES),
        10**9,
    )(mine, modes, consts, s1, s2, x, w_second)

    part = swap(g1rows, PLANE)
    (both,) = call(ring_kernel, [(n_z, share1 + bit2, ch)], [], 10**6)(part, mine)
    (whole,) = call(
        lambda *r: plane_kernel(share2, *r), [(n_pl // 2, share2 + share1, ch)], [((share2, LANES), F32)], 10**6
    )(swap(both, RING))
    whole = swap(whole, CHIPS)
    whole, g1 = lax.optimization_barrier((whole, g1))
    other = swap_cores(whole)
    grad_field, d_modes, spread_d, bias2 = call(
        lambda *r: field_kernel(float(nlat * nlon), *r),
        [(rows, cols, cin), modes.shape, (LANES, LANES), (1, LANES)],
        pair(N3),
        10**9,
    )(g1, w1_back, mine, modes, consts)
    grad_w_second, grad_w_first, grad_b_first = call(
        finish_kernel,
        [(9, ch, ch), (9, cin, ch), (1, ch)],
        [((2 * HALF, LANES), F32)],
        10**6,
        smem=(0,),
    )(core, whole, other, spread_d)
    return (grad_field.transpose(2, 0, 1), grad_w_first.transpose(0, 2, 1), grad_b_first[0], grad_w_second, bias2[0], d_modes)


def solution(mesh):
    fine = Mesh(mesh.devices.reshape(4, 2, 2, 16, 2), ("y", "xl", "c", "z", "xh"))
    in_specs = (P(None, LAT, LON), P(), P(), P(), P(), P(), P())
    out_specs = (P(None, LAT, LON), P(), P(), P(), P(), P())
    return jax.shard_map(body, mesh=fine, in_specs=in_specs, out_specs=out_specs, check_vma=False)
```
